256 devices in a mesh: cent: 4 (over y_lo, core), pts: 64 (over z, x, y_hi).
Axes of the slice: x: 4, y: 4 (y_hi: 2, y_lo: 2; y = y_hi * 2 + y_lo), z: 8, core: 2. Of those that a mesh axis runs over, the one named last changes fastest.
Arguments:
- points: bfloat16 [96, 32768], P(None, ('cent', 'pts')), may hold values from -60 to 60
- centroids: bfloat16 [96, 65536], P(None, 'cent'), may hold values from -6 to 6
Outputs:
- new_centroids: float32 [96, 65536], P(None, 'cent')
- normalizers: float32 [32768], P(('cent', 'pts'))
The draws below stay inside these ranges and needn't reach their ends.
All inputs are finite; a program needn't handle non-finite values.
Results may differ from the reference program's by a relative error of at most 0.0065.
The reference program's roundings to bfloat16 on the way (of `unit_cols` and `weights`) count: a program that leaves them out, or rounds other values in their place, can miss the bound.
Values may be sent and summed in bfloat16 or wider, within the bound.
A program may use at most 128 MiB of HBM per device.

```python
import jax
import jax.numpy as jnp
from jax import lax

D = 96
K = 65536
NPTS = 32768


def centroid_base(key):
    return jnp.clip(jax.random.normal(key, (D, K), jnp.float32), -6.0, 6.0)


def draw_centroids(key, part):
    raw_cols = centroid_base(key)
    return raw_cols.astype(jnp.bfloat16)


def draw_points(key, part):
    raw_cols = centroid_base(key)
    key = jax.random.fold_in(key, 5)
    subkeys = jax.random.split(key, 2)
    unit_cols = raw_cols / jnp.sqrt(jnp.sum(raw_cols * raw_cols, axis=0, keepdims=True))
    owners = jax.random.randint(subkeys[0], (NPTS,), 0, K)
    chosen = jnp.take(unit_cols, owners, axis=1)
    jitter = jnp.clip(jax.random.normal(subkeys[1], (D, NPTS), jnp.float32), -6.0, 6.0)
    vectors = 0.8 * chosen + 0.6 * jitter / jnp.sqrt(1.0 * D)
    return vectors.astype(jnp.bfloat16)


def setup_inputs(seed: int = 0) -> dict:
    seeds = jax.random.split(jax.random.key(seed), 3)
    return {
        "points": draw_points(jax.random.fold_in(seeds[2], 71), 0),
        "centroids": draw_centroids(jax.random.fold_in(seeds[2], 71), 0),
    }


def reference(points, centroids):
    as_float = centroids.astype(jnp.float32)
    unit_cols = (as_float * lax.rsqrt(lax.optimization_barrier(jnp.sum(as_float * as_float, axis=0, keepdims=True)) + 1e-06)).astype(jnp.bfloat16)
    unit_wide = unit_cols.astype(jnp.float32)
    row_block = 512 if NPTS % 512 == 0 else NPTS
    blocked = points.reshape(D, NPTS // row_block, row_block).transpose(1, 0, 2)

    def visit(carry, piece):
        sums_now, mass_now = carry
        piece_wide = piece.astype(jnp.float32)
        scores = 10.0 * jnp.dot(piece_wide.T, unit_wide, precision=lax.Precision.HIGHEST)
        highest = lax.optimization_barrier(jnp.max(scores, axis=1))
        log_norm = highest + jnp.log(lax.optimization_barrier(jnp.sum(jnp.exp(scores - highest[:, None]), axis=1)))
        weights = jnp.exp(scores - log_norm[:, None]).astype(jnp.bfloat16)
        weights_wide = weights.astype(jnp.float32)
        sums_now = sums_now + jnp.dot(piece_wide, weights_wide, precision=lax.Precision.HIGHEST)
        mass_now = mass_now + lax.optimization_barrier(jnp.sum(weights_wide, axis=0))
        return ((sums_now, mass_now), log_norm)
    start = (jnp.zeros((D, K), jnp.float32), jnp.zeros((K,), jnp.float32))
    (weighted_sums, masses), log_blocks = lax.scan(visit, start, blocked)
    new_centroids = (weighted_sums + 0.1 * unit_wide) / (masses + 0.1)[None, :]
    return (new_centroids, log_blocks.reshape(NPTS))
```

```python
import functools

import jax
import jax.numpy as jnp
from jax import lax
from jax.experimental import pallas as pl
from jax.experimental.pallas import tpu as pltpu
from jax.sharding import Mesh, PartitionSpec as P

TEMPER_SCALE = 10.0
PRIOR_MASS = 0.1
EPSILON = 1e-06
LOG2E = 1.4426950408889634
LN2 = 0.6931471805599453
AXES = ("yl", "core", "z", "x", "yh")
PLANE = ("yl", "core", "z", "yh")
GROUP = ("z", "x", "yh")
BIG = 2048


def unit_columns(centroids):
    as_float = centroids.astype(jnp.float32)
    return (
        as_float * lax.rsqrt(jnp.sum(as_float * as_float, axis=0, keepdims=True) + EPSILON)
    ).astype(jnp.bfloat16)


def stats_kernel(pts_ref, ut_ref, out_ref):
    cols, rows = pts_ref.shape[1], ut_ref.shape[0]
    step = 256

    def block(j, _):
        at = pl.ds(pl.multiple_of(j * BIG, BIG), BIG)
        pts = pts_ref[:, at]
        top = jnp.full((8, BIG), -1e30, jnp.float32)
        total = jnp.zeros((8, BIG), jnp.float32)
        for k in range(0, rows, step):
            s = jnp.dot(ut_ref[k : k + step, :], pts, preferred_element_type=jnp.float32)
            s = s.reshape(step // 8, 8, BIG)
            new = jnp.maximum(top, jnp.max(s, axis=0))
            e = jnp.exp2((s - new[None]) * (TEMPER_SCALE * LOG2E))
            total = total * jnp.exp2((top - new) * (TEMPER_SCALE * LOG2E)) + jnp.sum(e, axis=0)
            top = new
        best = jnp.max(top, axis=0, keepdims=True)
        out_ref[0:1, at] = best
        out_ref[1:2, at] = jnp.sum(
            total * jnp.exp2((top - best) * (TEMPER_SCALE * LOG2E)), axis=0, keepdims=True
        )
        return 0

    lax.fori_loop(0, cols // BIG, block, 0)


def sums_kernel(pts_ref, lse_ref, ut_ref, ptst_ref, out_ref, ext_ref):
    cols, rows = pts_ref.shape[1], ut_ref.shape[0]
    step = 256
    ext_ref[0:96, :] = pts_ref[...]
    a = lse_ref[...] * (-1.0 / TEMPER_SCALE)
    hi = a.astype(jnp.bfloat16).astype(jnp.float32)
    mid = (a - hi).astype(jnp.bfloat16).astype(jnp.float32)
    low = a - hi - mid
    row = lax.broadcasted_iota(jnp.int32, (32, cols), 0)
    extra = jnp.where(row == 0, hi, jnp.where(row == 1, mid, jnp.where(row == 2, low, 0.0)))
    ext_ref[96:128, :] = extra.astype(jnp.bfloat16)
    out_ref[...] = jnp.zeros_like(out_ref)

    def block(j, _):
        at = pl.ds(pl.multiple_of(j * BIG, BIG), BIG)
        pts = ext_ref[:, at]
        ptst = ptst_ref[at, :]
        for k in range(0, rows, step):
            s = jnp.dot(ut_ref[k : k + step, :], pts, preferred_element_type=jnp.float32)
            e = jnp.exp2(s * (TEMPER_SCALE * LOG2E)).astype(jnp.bfloat16)
            out_ref[k : k + step, :] += jnp.dot(e, ptst, preferred_element_type=jnp.float32)
        return 0

    lax.fori_loop(0, cols // BIG, block, 0)


def per_device(points, centroids):
    z, x, yh = lax.axis_index("z"), lax.axis_index("x"), lax.axis_index("yh")
    vmem = pl.BlockSpec(memory_space=pltpu.VMEM)
    params = pltpu.CompilerParams(vmem_limit_bytes=40 * 2**20)
    pts = lax.all_gather(points, PLANE, axis=1, tiled=True)
    mine = jnp.concatenate(
        [
            lax.dynamic_slice_in_dim(centroids, z * 2048 + k * 512 + yh * 256, 256, axis=1)
            for k in range(4)
        ],
        axis=1,
    )
    unit = unit_columns(mine)
    ut = unit.T
    cols, rows = pts.shape[1], ut.shape[0]
    stats = pl.pallas_call(
        stats_kernel,
        out_shape=jax.ShapeDtypeStruct((2, cols), jnp.float32),
        in_specs=[vmem, vmem],
        out_specs=vmem,
        compiler_params=params,
        name="stats",
    )(pts, ut)
    parts = lax.all_to_all(
        stats.reshape(2, 64, 128).transpose(1, 0, 2), PLANE, split_axis=0, concat_axis=0, tiled=True
    )
    best = jnp.max(parts[:, 0], axis=0)
    total = jnp.sum(
        parts[:, 1] * jnp.exp2((parts[:, 0] - best) * (TEMPER_SCALE * LOG2E)), axis=0
    )
    own_log = TEMPER_SCALE * best + jnp.log(total)
    logs = lax.all_gather(own_log, PLANE, axis=0, tiled=True)
    ones = jnp.ones((rows, 3), jnp.bfloat16)
    ut_ext = jnp.concatenate([ut, ones, jnp.zeros((rows, 29), jnp.bfloat16)], axis=1)
    ptst = jnp.concatenate(
        [pts.T, jnp.ones((cols, 1), jnp.bfloat16), jnp.zeros((cols, 31), jnp.bfloat16)], axis=1
    )
    sums = pl.pallas_call(
        sums_kernel,
        out_shape=jax.ShapeDtypeStruct((rows, 128), jnp.float32),
        in_specs=[vmem] * 4,
        out_specs=vmem,
        scratch_shapes=[pltpu.VMEM((128, cols), jnp.bfloat16)],
        compiler_params=params,
        name="sums",
    )(pts, logs.reshape(1, cols), ut_ext, ptst)
    sums = lax.psum_scatter(sums, "x", scatter_dimension=0, tiled=True)
    own_unit = lax.dynamic_slice_in_dim(unit, x * 256, 256, axis=1)
    fresh = (sums[:, :96].T + PRIOR_MASS * own_unit.astype(jnp.float32)) / (
        sums[:, 96] + PRIOR_MASS
    )[None, :]
    whole = lax.all_gather(fresh.astype(jnp.bfloat16), GROUP, axis=1, tiled=True)
    return (whole.astype(jnp.float32), own_log)


def solution(mesh):
    cube = Mesh(mesh.devices.reshape(2, 2, 8, 4, 2), AXES)
    return jax.shard_map(
        per_device,
        mesh=cube,
        in_specs=(P(None, AXES), P(None, ("yl", "core"))),
        out_specs=(P(None, ("yl", "core")), P(AXES)),
        check_vma=False,
    )
```

```python
import functools

import jax
import jax.numpy as jnp
from jax import lax
from jax.experimental import pallas as pl
from jax.experimental.pallas import tpu as pltpu
from jax.sharding import Mesh, PartitionSpec as P

TEMPER_SCALE = 10.0
PRIOR_MASS = 0.1
EPSILON = 1e-06
LOG2E = 1.4426950408889634
LN2 = 0.6931471805599453
SCALE = TEMPER_SCALE * LOG2E
AXES = ("yl", "core", "z", "x", "yh")
MESH = pl.DeviceIdType.MESH
D = 96
HALF = 2048
BF = jnp.bfloat16
F32 = jnp.float32


def em_kernel(
    points, cents, g, own_log,
    pg, cu, ut, ue, ptst, pe, lp, rxa, cb, rxb, lo, w, rxr,
    cu_sem, ps, pr, ds, dr, bs, br, rs, rr, zs, zr, xs, xr, fs, fr,
):
    yl, core, z, x, yh = [lax.axis_index(a) for a in AXES]
    y = yh * 2 + yl
    chip = x * 4 + y

    def at_plane(i):
        tx, ty = lax.rem(x + i // 4, 4), lax.rem(y + i % 4, 4)
        return (lax.rem(ty, 2), core, z, tx, ty // 2)

    def at_z(i):
        return (yl, core, lax.rem(z + i, 8), x, yh)

    def at_x(i):
        return (yl, core, z, lax.rem(x + i, 4), yh)

    other = (yl, 1 - core, z, x, yh)
    across = (yl, core, z, x, 1 - yh)

    def remote(src, dst, s, r, to):
        return pltpu.make_async_remote_copy(
            src_ref=src, dst_ref=dst, send_sem=s, recv_sem=r, device_id=to, device_id_type=MESH
        )

    loads = []
    for c in range(2):
        for k in range(8):
            col = pl.multiple_of(k * 2048 + (x * 2 + yh) * 256 + c * 128, 128)
            n = c * 8 + k
            cp = pltpu.make_async_copy(
                cents.at[:, pl.ds(col, 128)], cu.at[:, n * 128 : n * 128 + 128], cu_sem.at[n]
            )
            cp.start()
            loads.append(cp)

    barrier = pltpu.get_barrier_semaphore()
    peers = [at_plane(i) for i in range(1, 16)] + [other] + [at_z(i) for i in range(1, 8)]
    for to in peers:
        pl.semaphore_signal(barrier, inc=1, device_id=to, device_id_type=MESH)
    pl.semaphore_wait(barrier, len(peers))

    mine = pl.ds(pl.multiple_of(chip * 128, 128), 128)
    sends = []
    for i in range(1, 16):
        cp = remote(points, pg.at[core, :, mine], ps.at[i], pr.at[i], at_plane(i))
        cp.start()
        sends.append(cp)
    pg[core, :, mine] = points[...]

    for cp in loads:
        cp.wait()
    ue[D:128, :] = jnp.where(
        lax.broadcasted_iota(jnp.int32, (32, 2048), 0) < 3, 1.0, 0.0
    ).astype(BF)
    for k in range(0, 2048, 512):
        f = cu[:, k : k + 512].astype(F32)
        u = (f * lax.rsqrt(jnp.sum(f * f, axis=0, keepdims=True) + EPSILON)).astype(BF)
        ue[0:D, k : k + 512] = u
        full = jnp.concatenate([u.astype(F32), jnp.zeros((32, 512), F32)], axis=0)
        ut[k : k + 512, :] = full.T.astype(BF)

    for cp in sends:
        cp.wait()
    swap = remote(pg.at[core], pg.at[core], ds.at[0], dr.at[0], other)
    swap.start()

    def stats(h):
        pts = pg[h]
        top = jnp.full((8, HALF), -1e30, F32)
        total = jnp.zeros((8, HALF), F32)
        for k in range(0, 2048, 256):
            s = jnp.dot(ut[k : k + 256, 0:D], pts, preferred_element_type=F32)
            s = s.reshape(32, 8, HALF)
            new = jnp.maximum(top, jnp.max(s, axis=0))
            e = jnp.exp2((s - new[None]) * SCALE)
            total = total * jnp.exp2((top - new) * SCALE) + jnp.sum(e, axis=0)
            top = new
        best = jnp.max(top, axis=0, keepdims=True)
        sums = jnp.sum(total * jnp.exp2((top - best) * SCALE), axis=0, keepdims=True)
        lp[h] = best * SCALE + jnp.log2(sums)

    stats(core)
    swap.wait()
    stats(1 - core)

    give = remote(lp.at[1 - core], rxa, ds.at[1], dr.at[1], other)
    give.start()
    ones = jnp.where(lax.broadcasted_iota(jnp.int32, (16, HALF), 0) < 1, 1.0, 0.0).astype(BF)
    for h in range(2):
        pe[h, 0:D, :] = pg[h]
        pe[h, D:112, :] = ones
    give.wait()
    a, b = lp[core], rxa[...]
    top = jnp.maximum(a, b)
    cb[...] = top + jnp.log2(jnp.exp2(a - top) + jnp.exp2(b - top))
    sends = []
    for i in range(1, 16):
        cp = remote(cb, rxb.at[i], bs.at[i], br.at[i], at_plane(i))
        cp.start()
        sends.append(cp)
    rxb[0] = cb[...]
    for h in range(2):
        for k in range(0, HALF, 512):
            f = jnp.concatenate(
                [pg[h, :, k : k + 512].astype(F32), jnp.zeros((32, 512), F32)], axis=0
            )
            ptst[h * HALF + k : h * HALF + k + 512, :] = f.T.astype(BF)
    for cp in sends:
        cp.wait()
    top = rxb[0]
    for i in range(1, 16):
        top = jnp.maximum(top, rxb[i])
    total = jnp.exp2(rxb[0] - top)
    for i in range(1, 16):
        total = total + jnp.exp2(rxb[i] - top)
    lo[core] = top + jnp.log2(total)
    back = remote(lo.at[core], lo.at[core], ds.at[2], dr.at[2], other)
    back.start()
    own_log[...] = lo[core, :, mine] * LN2
    back.wait()

    row = lax.broadcasted_iota(jnp.int32, (32, 512), 0)
    for h in range(2):
        for k in range(0, HALF, 512):
            v = lo[h, :, k : k + 512] * (-1.0 / SCALE)
            hi = v.astype(BF).astype(F32)
            mid = (v - hi).astype(BF).astype(F32)
            low = v - hi - mid
            f = jnp.where(row == 0, hi, jnp.where(row == 1, mid, jnp.where(row == 2, low, 0.0)))
            ptst[h * HALF + k : h * HALF + k + 512, D:128] = f.T.astype(BF)

    def sums(c):
        for q in range(2):
            at = c * 1024 + q * 512
            uk = ue[:, at : at + 512]

            def block(j, acc):
                n = pl.ds(pl.multiple_of(j * 1024, 1024), 1024)
                m = pl.ds(pl.multiple_of(lax.rem(j, 2) * 1024, 1024), 1024)
                s = jnp.dot(ptst[n, :], uk, preferred_element_type=F32)
                e = jnp.exp2(s * SCALE).astype(BF)
                return acc + jnp.dot(pe[j // 2, :, m], e, preferred_element_type=F32)

            acc = lax.fori_loop(0, 4, block, jnp.zeros((112, 512), F32))
            for k in range(4):
                w[c, q * 4 + k] = acc[0:104, k * 128 : k * 128 + 128]

    def reduce_start(c):
        cps = []
        for i in (4, 3, 5, 2, 6, 1, 7):
            zz = lax.rem(z + i, 8)
            cp = remote(w.at[c, zz], rxr.at[c, i], rs.at[c, i], rr.at[c, i], at_z(i))
            cp.start()
            cps.append(cp)
        return cps

    def finish(c):
        acc = w[c, z]
        for i in range(1, 8):
            acc = acc + rxr[c, i]
        u = ue[0:D, pl.ds(pl.multiple_of(c * 1024 + z * 128, 128), 128)].astype(F32)
        g[c, x, yh, z] = ((acc[0:D] + PRIOR_MASS * u) / (acc[D : D + 1] + PRIOR_MASS)).astype(BF)

    def along_z(c):
        cps = []
        for i in (4, 3, 5, 2, 6, 1, 7):
            slot = g.at[c, x, yh, z]
            cp = remote(slot, slot, zs.at[c, i], zr.at[c, i], at_z(i))
            cp.start()
            cps.append(cp)
        return cps

    def region(c, xx, hh, s, r, to):
        cp = remote(g.at[c, xx, hh], g.at[c, xx, hh], s, r, to)
        cp.start()
        return cp

    def spread(c):
        first = region(c, x, yh, xs.at[c, 0], xr.at[c, 0], across)
        return [first] + [
            region(c, x, yh, xs.at[c, i], xr.at[c, i], at_x(i)) for i in (2, 1, 3)
        ]

    sums(0)
    red0 = reduce_start(0)
    sums(1)
    red1 = reduce_start(1)
    for cp in red0:
        cp.wait()
    finish(0)
    z0 = along_z(0)
    for cp in red1:
        cp.wait()
    finish(1)
    z1 = along_z(1)
    for cp in z0:
        cp.wait()
    s0 = spread(0)
    for cp in z1:
        cp.wait()
    s1 = spread(1)
    fwd = []
    s1[0].wait_recv()
    for i in (2, 1, 3):
        fwd.append(region(1, x, 1 - yh, fs.at[1, i], fr.at[1, i], at_x(i)))
    for n, i in ((2, 1), (3, 3), (1, 2)):
        s0[n].wait_recv()
        xx = lax.rem(x + 4 - i, 4)
        fwd.append(region(0, xx, yh, fs.at[0, i], fr.at[0, i], across))
    s0[0].wait_recv()
    for cp in s1[1:]:
        cp.wait_recv()
    for cp in s0 + s1:
        cp.wait_send()
    for cp in fwd:
        cp.wait()


def widen_kernel(g, out):
    for c in range(2):
        for hh in range(2):
            at = (hh * 2 + c) * 128
            out[:, at : at + 128] = g[c, 0, hh, 0].astype(F32)


def per_device(points, centroids):
    vmem = pl.BlockSpec(memory_space=pltpu.VMEM)
    dma = pltpu.SemaphoreType.DMA
    g, own_log = pl.pallas_call(
        em_kernel,
        out_shape=[
            jax.ShapeDtypeStruct((2, 4, 2, 8, D, 128), BF),
            jax.ShapeDtypeStruct((1, 128), F32),
        ],
        in_specs=[vmem, pl.BlockSpec(memory_space=pl.ANY)],
        out_specs=[vmem, vmem],
        scratch_shapes=[
            pltpu.VMEM((2, D, HALF), BF),
            pltpu.VMEM((D, 2048), BF),
            pltpu.VMEM((2048, 128), BF),
            pltpu.VMEM((128, 2048), BF),
            pltpu.VMEM((2 * HALF, 128), BF),
            pltpu.VMEM((2, 112, HALF), BF),
            pltpu.VMEM((2, 1, HALF), F32),
            pltpu.VMEM((1, HALF), F32),
            pltpu.VMEM((1, HALF), F32),
            pltpu.VMEM((16, 1, HALF), F32),
            pltpu.VMEM((2, 1, HALF), F32),
            pltpu.VMEM((2, 8, 104, 128), F32),
            pltpu.VMEM((2, 8, 104, 128), F32),
            dma((16,)), dma((16,)), dma((16,)), dma((3,)), dma((3,)), dma((16,)), dma((16,)),
            dma((2, 8)), dma((2, 8)), dma((2, 8)), dma((2, 8)), dma((2, 4)), dma((2, 4)),
            dma((2, 4)), dma((2, 4)),
        ],
        compiler_params=pltpu.CompilerParams(
            collective_id=0, has_side_effects=True, vmem_limit_bytes=48 * 2**20
        ),
        name="em",
    )(points, centroids)
    whole = pl.pallas_call(
        widen_kernel,
        grid=(8, 4),
        out_shape=jax.ShapeDtypeStruct((D, 16384), F32),
        in_specs=[pl.BlockSpec((2, 1, 2, 1, D, 128), lambda z, x: (0, x, 0, z, 0, 0))],
        out_specs=pl.BlockSpec((D, 512), lambda z, x: (0, z * 4 + x)),
        name="widen",
    )(g)
    return (whole, own_log.reshape(128))


def solution(mesh):
    cube = Mesh(mesh.devices.reshape(2, 2, 8, 4, 2), AXES)
    return jax.shard_map(
        per_device,
        mesh=cube,
        in_specs=(P(None, AXES), P(None, ("yl", "core"))),
        out_specs=(P(None, ("yl", "core")), P(AXES)),
        check_vma=False,
    )
```

```python
import functools

import jax
import jax.numpy as jnp
from jax import lax
from jax.experimental import pallas as pl
from jax.experimental.pallas import tpu as pltpu
from jax.sharding import Mesh, PartitionSpec as P

TEMPER_SCALE = 10.0
PRIOR_MASS = 0.1
EPSILON = 1e-06
LOG2E = 1.4426950408889634
LN2 = 0.6931471805599453
SCALE = TEMPER_SCALE * LOG2E
AXES = ("yl", "core", "z", "x", "yh")
MESH = pl.DeviceIdType.MESH
D = 96
HALF = 2048
BF = jnp.bfloat16
F32 = jnp.float32


def em_kernel(
    points, cents, g, own_log,
    stage, pg, cu, ut, ue, ptst, pe, lp, rxa, cb, rxb, lo, w, wb, rxr,
    cu_sem, ps, pr, ds, dr, bs, br, rs, rr, zs, zr, gs, gr,
):
    yl, core, z, x, yh = [lax.axis_index(a) for a in AXES]
    y = yh * 2 + yl
    chip = x * 4 + y

    def at_plane(i):
        tx, ty = lax.rem(x + i // 4, 4), lax.rem(y + i % 4, 4)
        return (lax.rem(ty, 2), core, z, tx, ty // 2)

    def at_z(i):
        return (yl, core, lax.rem(z + i, 8), x, yh)

    def at_x(i):
        return (yl, core, z, lax.rem(x + i, 4), yh)

    other = (yl, 1 - core, z, x, yh)
    across = (yl, core, z, x, 1 - yh)

    def remote(src, dst, s, r, to):
        return pltpu.make_async_remote_copy(
            src_ref=src, dst_ref=dst, send_sem=s, recv_sem=r, device_id=to, device_id_type=MESH
        )

    loads = []
    for c in range(2):
        for k in range(8):
            col = pl.multiple_of(k * 2048 + (x * 2 + yh) * 256 + c * 128, 128)
            n = c * 8 + k
            cp = pltpu.make_async_copy(
                cents.at[:, pl.ds(col, 128)], cu.at[:, n * 128 : n * 128 + 128], cu_sem.at[n]
            )
            cp.start()
            loads.append(cp)

    own = pltpu.make_async_copy(points, stage, cu_sem.at[16])
    own.start()
    barrier = pltpu.get_barrier_semaphore()
    peers = [at_plane(i) for i in range(1, 16)] + [other] + [at_z(i) for i in range(1, 8)]
    for to in peers:
        pl.semaphore_signal(barrier, inc=1, device_id=to, device_id_type=MESH)
    pl.semaphore_wait(barrier, len(peers))

    mine = pl.ds(pl.multiple_of(chip * 128, 128), 128)
    order = (1, 2, 3, 4, 5, 6, 7, 12, 13, 14, 15, 8, 9, 10, 11)
    own.wait()
    sends = {}
    for i in order:
        cp = remote(stage, pg.at[core, :, mine], ps.at[i], pr.at[i], at_plane(i))
        cp.start()
        sends[i] = cp
    pg[core, :, mine] = stage[...]

    for cp in loads:
        cp.wait()
    ue[D:128, :] = jnp.where(
        lax.broadcasted_iota(jnp.int32, (32, 2048), 0) < 3, 1.0, 0.0
    ).astype(BF)
    for k in range(0, 2048, 512):
        f = cu[:, k : k + 512].astype(F32)
        u = (f * lax.rsqrt(jnp.sum(f * f, axis=0, keepdims=True) + EPSILON)).astype(BF)
        ue[0:D, k : k + 512] = u
        full = jnp.concatenate([u.astype(F32), jnp.zeros((32, 512), F32)], axis=0)
        ut[k : k + 512, :] = full.T.astype(BF)

    def column(k):
        return pl.ds(pl.multiple_of(lax.rem(x + 4 - k, 4) * 512, 512), 512)

    def stats(h, k):
        pts = pg[h, :, column(k)]
        top = jnp.full((8, 512), -1e30, F32)
        total = jnp.zeros((8, 512), F32)
        for r in range(0, 2048, 256):
            s = jnp.dot(ut[r : r + 256, 0:D], pts, preferred_element_type=F32)
            s = s.reshape(32, 8, 512)
            new = jnp.maximum(top, jnp.max(s, axis=0))
            e = jnp.exp2((s - new[None]) * SCALE)
            total = total * jnp.exp2((top - new) * SCALE) + jnp.sum(e, axis=0)
            top = new
        best = jnp.max(top, axis=0, keepdims=True)
        sums = jnp.sum(total * jnp.exp2((top - best) * SCALE), axis=0, keepdims=True)
        lp[h, :, column(k)] = best * SCALE + jnp.log2(sums)

    swaps, before = [], None
    for n, k in enumerate((0, 1, 3, 2)):
        for i in range(4 * k, 4 * k + 4):
            if i:
                sends[i].wait_recv()
        part = pg.at[core, :, column(k)]
        swap = remote(part, part, ds.at[3 + n], dr.at[3 + n], other)
        swap.start()
        if before is not None:
            swaps[-1].wait_recv()
            stats(1 - core, before)
        swaps.append(swap)
        stats(core, k)
        before = k
    swaps[-1].wait_recv()
    stats(1 - core, before)
    for cp in list(sends.values()) + swaps:
        cp.wait_send()

    give = remote(lp.at[1 - core], rxa, ds.at[1], dr.at[1], other)
    give.start()
    ones = jnp.where(lax.broadcasted_iota(jnp.int32, (16, HALF), 0) < 2, 1.0, 0.0).astype(BF)
    for h in range(2):
        pe[h, 0:D, :] = pg[h]
        pe[h, D:112, :] = ones
    give.wait()
    a, b = lp[core], rxa[...]
    top = jnp.maximum(a, b)
    cb[...] = top + jnp.log2(jnp.exp2(a - top) + jnp.exp2(b - top))
    sends = []
    for i in range(1, 16):
        cp = remote(cb, rxb.at[i], bs.at[i], br.at[i], at_plane(i))
        cp.start()
        sends.append(cp)
    rxb[0] = cb[...]
    for h in range(2):
        for k in range(0, HALF, 512):
            f = jnp.concatenate(
                [pg[h, :, k : k + 512].astype(F32), jnp.zeros((32, 512), F32)], axis=0
            )
            ptst[h * HALF + k : h * HALF + k + 512, :] = f.T.astype(BF)
    for cp in sends:
        cp.wait()
    top = rxb[0]
    for i in range(1, 16):
        top = jnp.maximum(top, rxb[i])
    total = jnp.exp2(rxb[0] - top)
    for i in range(1, 16):
        total = total + jnp.exp2(rxb[i] - top)
    lo[core] = top + jnp.log2(total)
    back = remote(lo.at[core], lo.at[core], ds.at[2], dr.at[2], other)
    back.start()
    own_log[...] = lo[core, :, mine] * LN2
    back.wait()

    row = lax.broadcasted_iota(jnp.int32, (32, 512), 0)
    for h in range(2):
        for k in range(0, HALF, 512):
            v = lo[h, :, k : k + 512] * (-1.0 / SCALE)
            hi = v.astype(BF).astype(F32)
            mid = (v - hi).astype(BF).astype(F32)
            low = v - hi - mid
            f = jnp.where(row == 0, hi, jnp.where(row == 1, mid, jnp.where(row == 2, low, 0.0)))
            ptst[h * HALF + k : h * HALF + k + 512, D:128] = f.T.astype(BF)

    def sums(c):
        for q in range(2):
            at = c * 1024 + q * 512
            uk = ue[:, at : at + 512]

            def block(j, acc):
                n = pl.ds(pl.multiple_of(j * 1024, 1024), 1024)
                m = pl.ds(pl.multiple_of(lax.rem(j, 2) * 1024, 1024), 1024)
                s = jnp.dot(ptst[n, :], uk, preferred_element_type=F32)
                e = jnp.exp2(s * SCALE).astype(BF)
                return acc + jnp.dot(pe[j // 2, :, m], e, preferred_element_type=F32)

            acc = lax.fori_loop(0, 4, block, jnp.zeros((112, 512), F32))
            tail = acc[D:112]
            hi = tail.astype(BF).astype(F32)
            first = lax.broadcasted_iota(jnp.int32, (16, 512), 0) == 0
            parts = jnp.where(first, hi, tail - hi).astype(BF)
            for k in range(4):
                at = slice(k * 128, k * 128 + 128)
                w[c, q * 4 + k] = acc[0:104, at]
                wb[c, q * 4 + k, 0:D] = acc[0:D, at].astype(BF)
                wb[c, q * 4 + k, D:112] = parts[:, at]

    def reduce_start(c):
        cps = []
        for i in (4, 3, 5, 2, 6, 1, 7):
            zz = lax.rem(z + i, 8)
            cp = remote(wb.at[c, zz], rxr.at[c, i], rs.at[c, i], rr.at[c, i], at_z(i))
            cp.start()
            cps.append(cp)
        return cps

    def finish(c):
        acc = w[c, z]
        for i in range(1, 8):
            acc = acc + rxr[c, i, 0:104].astype(F32)
        sums, mass = acc[0:D], acc[D : D + 1] + (acc[D + 1 : D + 2] - w[c, z, D + 1 : D + 2])
        u = ue[0:D, pl.ds(pl.multiple_of(c * 1024 + z * 128, 128), 128)].astype(F32)
        g[c, x, yh, z] = ((sums + PRIOR_MASS * u) / (mass + PRIOR_MASS)).astype(BF)

    def along_z(c):
        cps = {}
        for i in (1, 7, 2, 6, 3, 5, 4):
            slot = g.at[c, x, yh, z]
            cp = remote(slot, slot, zs.at[c, i], zr.at[c, i], at_z(i))
            cp.start()
            cps[i] = cp
        return cps

    pushed = {}

    def push(c, i, dx, dh, to, rdx, rdh):
        slot = g.at[c, lax.rem(x + 4 - dx, 4), lax.rem(yh + dh, 2), lax.rem(z + 8 - i, 8)]
        cp = remote(slot, slot, gs.at[c, rdh, rdx, i], gr.at[c, rdh, rdx, i], to)
        cp.start()
        pushed[c, i, rdx, rdh] = cp

    def arrived(c, i, dx, dh):
        pushed[c, i, dx, dh].wait_recv()

    right, left = at_x(1), at_x(3)

    def step1(c, j, i):
        if i:
            zc[c][i].wait_recv()
        push(c, i, 0, 0, across, 0, 1)
        push(c, i, 0, 0, right, 1, 0)
        push(c, i, 0, 0, left, 3, 0)

    def y_last(c, j):
        return j % 2 == 0 and not (c == 1 and j == 6)

    def relay(c, j, i, dh):
        arrived(c, i, 1, dh)
        if j // 2 % 2 == 0:
            push(c, i, 1, dh, right, 2, dh)
        arrived(c, i, 3, dh)
        if j // 2 % 2 == 1:
            push(c, i, 3, dh, left, 2, dh)

    def step2(c, j, i):
        relay(c, j, i, 0)
        if y_last(c, j):
            push(c, i, 1, 0, across, 1, 1)
            push(c, i, 3, 0, across, 3, 1)
        arrived(c, i, 0, 1)
        if not y_last(c, j):
            push(c, i, 0, 1, right, 1, 1)
            push(c, i, 0, 1, left, 3, 1)

    def step3(c, j, i):
        arrived(c, i, 2, 0)
        if y_last(c, j):
            push(c, i, 2, 0, across, 2, 1)
            arrived(c, i, 1, 1)
            arrived(c, i, 3, 1)
        else:
            relay(c, j, i, 1)

    def step4(c, j, i):
        arrived(c, i, 2, 1)

    zc = {}

    def begin(c):
        for cp in red[c]:
            cp.wait()
        finish(c)
        zc[c] = along_z(c)

    events = [(4.9, 0, begin, (1,))]
    for c in range(2):
        for j, i in enumerate((0, 1, 7, 2, 6, 3, 5, 4)):
            for n, step in enumerate((step1, step2, step3, step4)):
                events.append((5 * c + j + 3 * n, n, step, (c, j, i)))
    events.sort(key=lambda e: (e[0], -e[1]))

    red = {}
    sums(0)
    red[0] = reduce_start(0)
    sums(1)
    red[1] = reduce_start(1)
    begin(0)
    for _, _, call, args in events:
        call(*args)
    for c in range(2):
        for cp in zc[c].values():
            cp.wait_send()
    for cp in pushed.values():
        cp.wait_send()


def widen_kernel(g, out):
    z = pl.program_id(0)
    for c in range(2):
        for xx in range(4):
            for hh in range(2):
                at = (xx * 4 + hh * 2 + c) * 128
                out[:, at : at + 128] = g[c, xx, hh, z].astype(F32)


def per_device(points, centroids):
    vmem = pl.BlockSpec(memory_space=pltpu.VMEM)
    dma = pltpu.SemaphoreType.DMA
    g, own_log = pl.pallas_call(
        em_kernel,
        out_shape=[
            jax.ShapeDtypeStruct((2, 4, 2, 8, D, 128), BF),
            jax.ShapeDtypeStruct((1, 128), F32),
        ],
        in_specs=[pl.BlockSpec(memory_space=pltpu.HBM)] * 2,
        out_specs=[vmem, vmem],
        scratch_shapes=[
            pltpu.VMEM((D, 128), BF),
            pltpu.VMEM((2, D, HALF), BF),
            pltpu.VMEM((D, 2048), BF),
            pltpu.VMEM((2048, 128), BF),
            pltpu.VMEM((128, 2048), BF),
            pltpu.VMEM((2 * HALF, 128), BF),
            pltpu.VMEM((2, 112, HALF), BF),
            pltpu.VMEM((2, 1, HALF), F32),
            pltpu.VMEM((1, HALF), F32),
            pltpu.VMEM((1, HALF), F32),
            pltpu.VMEM((16, 1, HALF), F32),
            pltpu.VMEM((2, 1, HALF), F32),
            pltpu.VMEM((2, 8, 104, 128), F32),
            pltpu.VMEM((2, 8, 112, 128), BF),
            pltpu.VMEM((2, 8, 112, 128), BF),
            dma((17,)), dma((16,)), dma((16,)), dma((7,)), dma((7,)), dma((16,)), dma((16,)),
            dma((2, 8)), dma((2, 8)), dma((2, 8)), dma((2, 8)), dma((2, 2, 4, 8)), dma((2, 2, 4, 8)),
        ],
        compiler_params=pltpu.CompilerParams(
            collective_id=0, has_side_effects=True, vmem_limit_bytes=48 * 2**20
        ),
        name="em",
    )(points, centroids)
    whole = pl.pallas_call(
        widen_kernel,
        grid=(8,),
        out_shape=jax.ShapeDtypeStruct((D, 16384), F32),
        in_specs=[vmem],
        out_specs=pl.BlockSpec((D, 2048), lambda z: (0, z)),
        compiler_params=pltpu.CompilerParams(vmem_limit_bytes=8 * 2**20),
        name="widen",
    )(g)
    return (whole, own_log.reshape(128))


def solution(mesh):
    cube = Mesh(mesh.devices.reshape(2, 2, 8, 4, 2), AXES)
    return jax.shard_map(
        per_device,
        mesh=cube,
        in_specs=(P(None, AXES), P(None, ("yl", "core"))),
        out_specs=(P(None, ("yl", "core")), P(AXES)),
        check_vma=False,
    )
```

```python
import functools

import jax
import jax.numpy as jnp
from jax import lax
from jax.experimental import pallas as pl
from jax.experimental.pallas import tpu as pltpu
from jax.sharding import Mesh, PartitionSpec as P

TEMPER_SCALE = 10.0
PRIOR_MASS = 0.1
EPSILON = 1e-06
LOG2E = 1.4426950408889634
LN2 = 0.6931471805599453
SCALE = TEMPER_SCALE * LOG2E
AXES = ("yl", "core", "z", "x", "yh")
MESH = pl.DeviceIdType.MESH
D = 96
ARRIVAL = (0, 1, 7, 2, 6, 3, 5, 4)
GROUP = 2
HALF = 2048
BF = jnp.bfloat16
F32 = jnp.float32


def em_kernel(
    points, cents, g, own_log,
    stage, pg, cu, ut, ue, ptst, pe, lp, rxa, cb, rxb, lo, w, wb, rxr,
    cu_sem, ps, pr, ds, dr, bs, br, rs, rr, zs, zr, gs, gr,
):
    yl, core, z, x, yh = [lax.axis_index(a) for a in AXES]
    y = yh * 2 + yl
    chip = x * 4 + y

    def at_plane(i):
        tx, ty = lax.rem(x + i // 4, 4), lax.rem(y + i % 4, 4)
        return (lax.rem(ty, 2), core, z, tx, ty // 2)

    def at_z(i):
        return (yl, core, lax.rem(z + i, 8), x, yh)

    def at_x(i):
        return (yl, core, z, lax.rem(x + i, 4), yh)

    other = (yl, 1 - core, z, x, yh)
    across = (yl, core, z, x, 1 - yh)

    def remote(src, dst, s, r, to):
        return pltpu.make_async_remote_copy(
            src_ref=src, dst_ref=dst, send_sem=s, recv_sem=r, device_id=to, device_id_type=MESH
        )

    loads = []
    for c in range(2):
        for k in range(8):
            col = pl.multiple_of(k * 2048 + (x * 2 + yh) * 256 + c * 128, 128)
            n = c * 8 + k
            cp = pltpu.make_async_copy(
                cents.at[:, pl.ds(col, 128)], cu.at[:, n * 128 : n * 128 + 128], cu_sem.at[n]
            )
            cp.start()
            loads.append(cp)

    own = pltpu.make_async_copy(points, stage, cu_sem.at[16])
    own.start()
    barrier = pltpu.get_barrier_semaphore()
    peers = [at_plane(i) for i in range(1, 16)] + [other] + [at_z(i) for i in range(1, 8)]
    for to in peers:
        pl.semaphore_signal(barrier, inc=1, device_id=to, device_id_type=MESH)
    for cp in loads:
        cp.wait()
    ue[D:128, :] = jnp.where(
        lax.broadcasted_iota(jnp.int32, (32, 2048), 0) < 3, 1.0, 0.0
    ).astype(BF)
    for k in range(0, 2048, 512):
        f = cu[:, k : k + 512].astype(F32)
        u = (f * lax.rsqrt(jnp.sum(f * f, axis=0, keepdims=True) + EPSILON)).astype(BF)
        ue[0:D, k : k + 512] = u
        full = jnp.concatenate([u.astype(F32), jnp.zeros((32, 512), F32)], axis=0)
        ut[k : k + 512, :] = full.T.astype(BF)
    pl.semaphore_wait(barrier, len(peers))

    mine = pl.ds(pl.multiple_of(chip * 128, 128), 128)
    order = (1, 2, 3, 4, 5, 6, 7, 12, 13, 14, 15, 8, 9, 10, 11)
    own.wait()
    sends = {}
    for i in order:
        cp = remote(stage, pg.at[core, :, mine], ps.at[i], pr.at[i], at_plane(i))
        cp.start()
        sends[i] = cp
    pg[core, :, mine] = stage[...]

    def column(k):
        return pl.ds(pl.multiple_of(lax.rem(x + 4 - k, 4) * 512, 512), 512)

    def stats(h, k):
        pts = pg[h, :, column(k)]
        top = jnp.full((8, 512), -1e30, F32)
        total = jnp.zeros((8, 512), F32)
        for r in range(0, 2048, 128):
            s = jnp.dot(ut[r : r + 128, 0:D], pts, preferred_element_type=F32)
            s = s.reshape(16, 8, 512)
            new = jnp.maximum(top, jnp.max(s, axis=0))
            e = jnp.exp2((s - new[None]) * SCALE)
            total = total * jnp.exp2((top - new) * SCALE) + jnp.sum(e, axis=0)
            top = new
        best = jnp.max(top, axis=0, keepdims=True)
        sums = jnp.sum(total * jnp.exp2((top - best) * SCALE), axis=0, keepdims=True)
        lp[h, :, column(k)] = best * SCALE + jnp.log2(sums)

    swaps, before = [], None
    for n, k in enumerate((0, 1, 3, 2)):
        for i in range(4 * k, 4 * k + 4):
            if i:
                sends[i].wait_recv()
        part = pg.at[core, :, column(k)]
        swap = remote(part, part, ds.at[3 + n], dr.at[3 + n], other)
        swap.start()
        if before is not None:
            swaps[-1].wait_recv()
            stats(1 - core, before)
        swaps.append(swap)
        stats(core, k)
        before = k
    swaps[-1].wait_recv()
    stats(1 - core, before)
    for cp in list(sends.values()) + swaps:
        cp.wait_send()

    give = remote(lp.at[1 - core], rxa, ds.at[1], dr.at[1], other)
    give.start()
    ones = jnp.where(lax.broadcasted_iota(jnp.int32, (16, HALF), 0) < 2, 1.0, 0.0).astype(BF)
    for h in range(2):
        pe[h, 0:D, :] = pg[h]
        pe[h, D:112, :] = ones
    give.wait()
    a, b = lp[core], rxa[...]
    top = jnp.maximum(a, b)
    cb[...] = top + jnp.log2(jnp.exp2(a - top) + jnp.exp2(b - top))
    sends = []
    for i in range(1, 16):
        cp = remote(cb, rxb.at[i], bs.at[i], br.at[i], at_plane(i))
        cp.start()
        sends.append(cp)
    rxb[0] = cb[...]
    for h in range(2):
        for k in range(0, HALF, 512):
            f = jnp.concatenate(
                [pg[h, :, k : k + 512].astype(F32), jnp.zeros((32, 512), F32)], axis=0
            )
            ptst[h * HALF + k : h * HALF + k + 512, :] = f.T.astype(BF)
    for cp in sends:
        cp.wait()
    top = rxb[0]
    for i in range(1, 16):
        top = jnp.maximum(top, rxb[i])
    total = jnp.exp2(rxb[0] - top)
    for i in range(1, 16):
        total = total + jnp.exp2(rxb[i] - top)
    lo[core] = top + jnp.log2(total)
    back = remote(lo.at[core], lo.at[core], ds.at[2], dr.at[2], other)
    back.start()
    own_log[...] = lo[core, :, mine] * LN2
    back.wait()

    row = lax.broadcasted_iota(jnp.int32, (32, 512), 0)
    for h in range(2):
        for k in range(0, HALF, 512):
            v = lo[h, :, k : k + 512] * (-1.0 / SCALE)
            hi = v.astype(BF).astype(F32)
            mid = (v - hi).astype(BF).astype(F32)
            low = v - hi - mid
            f = jnp.where(row == 0, hi, jnp.where(row == 1, mid, jnp.where(row == 2, low, 0.0)))
            ptst[h * HALF + k : h * HALF + k + 512, D:128] = f.T.astype(BF)

    first = lax.broadcasted_iota(jnp.int32, (16, 512), 0) == 0

    def owner(c, i):
        return pl.ds(pl.multiple_of(c * 1024 + lax.rem(z + i, 8) * 128, 128), 128)

    def sums(c):
        cps = []
        for near in ((4, 3, 5, 2), (6, 1, 7, 0)):
            uk = jnp.concatenate([ue[:, owner(c, i)] for i in near], axis=1)
            acc = jnp.zeros((112, 512), F32)
            for h in range(2):
                s = jnp.dot(ptst[h * HALF : h * HALF + HALF, :], uk, preferred_element_type=F32)
                e = jnp.exp2(s * SCALE).astype(BF)
                acc = acc + jnp.dot(pe[h], e, preferred_element_type=F32)
            tail = acc[D:112]
            hi = tail.astype(BF).astype(F32)
            parts = jnp.where(first, hi, tail - hi).astype(BF)
            for k, i in enumerate(near):
                at = slice(k * 128, k * 128 + 128)
                if i == 0:
                    w[c] = acc[0:104, at]
                    continue
                wb[c, i, 0:D] = acc[0:D, at].astype(BF)
                wb[c, i, D:112] = parts[:, at]
                cp = remote(wb.at[c, i], rxr.at[c, i], rs.at[c, i], rr.at[c, i], at_z(i))
                cp.start()
                cps.append(cp)
        return cps

    def finish(c):
        acc = w[c]
        for i in range(1, 8):
            acc = acc + rxr[c, i, 0:104].astype(F32)
        sums, mass = acc[0:D], acc[D : D + 1] + (acc[D + 1 : D + 2] - w[c, D + 1 : D + 2])
        u = ue[0:D, owner(c, 0)].astype(F32)
        g[c, 0, 0, 0] = ((sums + PRIOR_MASS * u) / (mass + PRIOR_MASS)).astype(BF)

    def along_z(c):
        cps = {}
        for j in range(1, 8):
            slot = g.at[c, 0, 0, j]
            cp = remote(g.at[c, 0, 0, 0], slot, zs.at[c, j], zr.at[c, j], at_z(ARRIVAL[j]))
            cp.start()
            cps[j] = cp
        return cps

    pushed = {}

    def push(c, n, dx, dh, to, rdx, rdh):
        js = pl.ds(n * GROUP, GROUP)
        cp = remote(
            g.at[c, dh, dx, js], g.at[c, rdh, rdx, js], gs.at[c, rdh, rdx, n], gr.at[c, rdh, rdx, n], to
        )
        cp.start()
        pushed[c, n, rdx, rdh] = cp

    def arrived(c, n, dx, dh):
        pushed[c, n, dx, dh].wait_recv()

    right, left = at_x(1), at_x(3)

    def y_last(c, n):
        return n % 2 == 0

    def relay(c, n, dh):
        if (c + n) % 2 == 0:
            arrived(c, n, 1, dh)
            push(c, n, 1, dh, right, 2, dh)
            arrived(c, n, 3, dh)
        else:
            arrived(c, n, 3, dh)
            push(c, n, 3, dh, left, 2, dh)
            arrived(c, n, 1, dh)

    def step1(c, n):
        for j in range(n * GROUP, n * GROUP + GROUP):
            if j:
                zc[c][j].wait_recv()
        push(c, n, 0, 0, across, 0, 1)
        push(c, n, 0, 0, right, 1, 0)
        push(c, n, 0, 0, left, 3, 0)

    def step2(c, n):
        relay(c, n, 0)
        if y_last(c, n):
            push(c, n, 1, 0, across, 1, 1)
            push(c, n, 3, 0, across, 3, 1)
        arrived(c, n, 0, 1)
        if not y_last(c, n):
            push(c, n, 0, 1, right, 1, 1)
            push(c, n, 0, 1, left, 3, 1)

    def step3(c, n):
        arrived(c, n, 2, 0)
        if y_last(c, n):
            push(c, n, 2, 0, across, 2, 1)
            arrived(c, n, 1, 1)
            arrived(c, n, 3, 1)
        else:
            relay(c, n, 1)

    def step4(c, n):
        arrived(c, n, 2, 1)

    zc = {}

    def begin(c):
        for cp in red[c]:
            cp.wait()
        finish(c)
        zc[c] = along_z(c)

    events = [(4.9, 0, begin, (1,))]
    for c in range(2):
        for n in range(8 // GROUP):
            for k, step in enumerate((step1, step2, step3, step4)):
                events.append((5 * c + GROUP * n + 6 * k, k, step, (c, n)))
    events.sort(key=lambda e: (e[0], -e[1]))

    red = {}
    red[0] = sums(0)
    red[1] = sums(1)
    begin(0)
    for _, _, call, args in events:
        call(*args)
    for c in range(2):
        for cp in zc[c].values():
            cp.wait_send()
    for cp in pushed.values():
        cp.wait_send()


def widen_kernel(g, log, out, log_out, buf, sem):
    mz, mx, mh = lax.axis_index("z"), lax.axis_index("x"), lax.axis_index("yh")
    cps = []
    for z in range(8):
        i = lax.rem(mz + 8 - z, 8)
        j = jnp.where(i == 0, 0, jnp.where(i <= 4, 2 * i - 1, 16 - 2 * i))
        for xx in range(4):
            dx = lax.rem(mx + 4 - xx, 4)
            for k in range(4):
                dh = lax.rem(mh + k // 2, 2)
                at = (z * 16 + xx * 4 + k) * 128
                buf[:, at : at + 128] = g[k % 2, dh, dx, j].astype(F32)
        at = slice(z * 2048, z * 2048 + 2048)
        cp = pltpu.make_async_copy(buf.at[:, at], out.at[:, at], sem.at[z])
        cp.start()
        cps.append(cp)
    log_out[...] = log[0]
    for cp in cps:
        cp.wait()


def per_device(points, centroids):
    vmem = pl.BlockSpec(memory_space=pltpu.VMEM)
    dma = pltpu.SemaphoreType.DMA
    g, own_log = pl.pallas_call(
        em_kernel,
        out_shape=[
            jax.ShapeDtypeStruct((2, 2, 4, 8, D, 128), BF),
            jax.ShapeDtypeStruct((1, 128), F32),
        ],
        in_specs=[pl.BlockSpec(memory_space=pltpu.HBM)] * 2,
        out_specs=[vmem, vmem],
        scratch_shapes=[
            pltpu.VMEM((D, 128), BF),
            pltpu.VMEM((2, D, HALF), BF),
            pltpu.VMEM((D, 2048), BF),
            pltpu.VMEM((2048, 128), BF),
            pltpu.VMEM((128, 2048), BF),
            pltpu.VMEM((2 * HALF, 128), BF),
            pltpu.VMEM((2, 112, HALF), BF),
            pltpu.VMEM((2, 1, HALF), F32),
            pltpu.VMEM((1, HALF), F32),
            pltpu.VMEM((1, HALF), F32),
            pltpu.VMEM((16, 1, HALF), F32),
            pltpu.VMEM((2, 1, HALF), F32),
            pltpu.VMEM((2, 104, 128), F32),
            pltpu.VMEM((2, 8, 112, 128), BF),
            pltpu.VMEM((2, 8, 112, 128), BF),
            dma((17,)), dma((16,)), dma((16,)), dma((7,)), dma((7,)), dma((16,)), dma((16,)),
            dma((2, 8)), dma((2, 8)), dma((2, 8)), dma((2, 8)), dma((2, 2, 4, 8 // GROUP)), dma((2, 2, 4, 8 // GROUP)),
        ],
        compiler_params=pltpu.CompilerParams(
            collective_id=0, has_side_effects=True, vmem_limit_bytes=48 * 2**20
        ),
        name="em",
    )(points, centroids)
    return pl.pallas_call(
        widen_kernel,
        out_shape=[
            jax.ShapeDtypeStruct((D, 16384), F32),
            jax.ShapeDtypeStruct((128,), F32),
        ],
        in_specs=[vmem, vmem],
        out_specs=[pl.BlockSpec(memory_space=pltpu.HBM), vmem],
        scratch_shapes=[pltpu.VMEM((D, 16384), F32), dma((8,))],
        compiler_params=pltpu.CompilerParams(vmem_limit_bytes=12 * 2**20),
        name="widen",
    )(g, own_log)


def solution(mesh):
    cube = Mesh(mesh.devices.reshape(2, 2, 8, 4, 2), AXES)
    return jax.shard_map(
        per_device,
        mesh=cube,
        in_specs=(P(None, AXES), P(None, ("yl", "core"))),
        out_specs=(P(None, ("yl", "core")), P(AXES)),
        check_vma=False,
    )
```

```python
import functools

import jax
import jax.numpy as jnp
from jax import lax
from jax.experimental import pallas as pl
from jax.experimental.pallas import tpu as pltpu
from jax.sharding import Mesh, PartitionSpec as P

TEMPER_SCALE = 10.0
PRIOR_MASS = 0.1
EPSILON = 1e-06
LOG2E = 1.4426950408889634
LN2 = 0.6931471805599453
SCALE = TEMPER_SCALE * LOG2E
AXES = ("yl", "core", "z", "x", "yh")
MESH = pl.DeviceIdType.MESH
D = 96
ARRIVAL = (0, 1, 7, 2, 6, 3, 5, 4)
GROUP = 2
RA = 32
HALF = 2048
BF = jnp.bfloat16
F32 = jnp.float32


def em_kernel(
    points, cents, ga, g, own_log,
    stage, pg, cu, ut, ue, ptst, pe, lp, rxa, cb, rxb, lo, w, wb, rxr,
    cu_sem, ps, pr, ds, dr, bs, br, rs, rr, zs, zr, gs, gr, as_, ar, rs_, rr_,
):
    yl, core, z, x, yh = [lax.axis_index(a) for a in AXES]
    y = yh * 2 + yl
    chip = x * 4 + y

    def at_plane(i):
        tx, ty = lax.rem(x + i // 4, 4), lax.rem(y + i % 4, 4)
        return (lax.rem(ty, 2), core, z, tx, ty // 2)

    def at_z(i):
        return (yl, core, lax.rem(z + i, 8), x, yh)

    def at_x(i):
        return (yl, core, z, lax.rem(x + i, 4), yh)

    other = (yl, 1 - core, z, x, yh)
    across = (yl, core, z, x, 1 - yh)

    def remote(src, dst, s, r, to):
        return pltpu.make_async_remote_copy(
            src_ref=src, dst_ref=dst, send_sem=s, recv_sem=r, device_id=to, device_id_type=MESH
        )

    loads = []
    for c in range(2):
        for k in range(8):
            col = pl.multiple_of(k * 2048 + (x * 2 + yh) * 256 + c * 128, 128)
            n = c * 8 + k
            cp = pltpu.make_async_copy(
                cents.at[:, pl.ds(col, 128)], cu.at[:, n * 128 : n * 128 + 128], cu_sem.at[n]
            )
            cp.start()
            loads.append(cp)

    own = pltpu.make_async_copy(points, stage, cu_sem.at[16])
    own.start()
    barrier = pltpu.get_barrier_semaphore()
    peers = [at_plane(i) for i in range(1, 16)] + [other] + [at_z(i) for i in range(1, 8)]
    for to in peers:
        pl.semaphore_signal(barrier, inc=1, device_id=to, device_id_type=MESH)
    for cp in loads:
        cp.wait()
    ue[D:128, :] = jnp.where(
        lax.broadcasted_iota(jnp.int32, (32, 2048), 0) < 3, 1.0, 0.0
    ).astype(BF)
    for k in range(0, 2048, 512):
        f = cu[:, k : k + 512].astype(F32)
        u = (f * lax.rsqrt(jnp.sum(f * f, axis=0, keepdims=True) + EPSILON)).astype(BF)
        ue[0:D, k : k + 512] = u
        full = jnp.concatenate([u.astype(F32), jnp.zeros((32, 512), F32)], axis=0)
        ut[k : k + 512, :] = full.T.astype(BF)
    pl.semaphore_wait(barrier, len(peers))

    mine = pl.ds(pl.multiple_of(chip * 128, 128), 128)
    order = (1, 2, 3, 4, 5, 6, 7, 12, 13, 14, 15, 8, 9, 10, 11)
    own.wait()
    sends = {}
    for i in order:
        cp = remote(stage, pg.at[core, :, mine], ps.at[i], pr.at[i], at_plane(i))
        cp.start()
        sends[i] = cp
    pg[core, :, mine] = stage[...]

    def column(k):
        return pl.ds(pl.multiple_of(lax.rem(x + 4 - k, 4) * 512, 512), 512)

    def stats(h, k):
        pts = pg[h, :, column(k)]
        top = jnp.full((8, 512), -1e30, F32)
        total = jnp.zeros((8, 512), F32)
        for r in range(0, 2048, 128):
            s = jnp.dot(ut[r : r + 128, 0:D], pts, preferred_element_type=F32)
            s = s.reshape(16, 8, 512)
            new = jnp.maximum(top, jnp.max(s, axis=0))
            e = jnp.exp2((s - new[None]) * SCALE)
            total = total * jnp.exp2((top - new) * SCALE) + jnp.sum(e, axis=0)
            top = new
        best = jnp.max(top, axis=0, keepdims=True)
        sums = jnp.sum(total * jnp.exp2((top - best) * SCALE), axis=0, keepdims=True)
        lp[h, :, column(k)] = best * SCALE + jnp.log2(sums)

    swaps, before = [], None
    for n, k in enumerate((0, 1, 3, 2)):
        for i in range(4 * k, 4 * k + 4):
            if i:
                sends[i].wait_recv()
        part = pg.at[core, :, column(k)]
        swap = remote(part, part, ds.at[3 + n], dr.at[3 + n], other)
        swap.start()
        if before is not None:
            swaps[-1].wait_recv()
            stats(1 - core, before)
        swaps.append(swap)
        stats(core, k)
        before = k
    swaps[-1].wait_recv()
    stats(1 - core, before)
    for cp in list(sends.values()) + swaps:
        cp.wait_send()

    give = remote(lp.at[1 - core], rxa, ds.at[1], dr.at[1], other)
    give.start()
    ones = jnp.where(lax.broadcasted_iota(jnp.int32, (16, HALF), 0) < 2, 1.0, 0.0).astype(BF)
    for h in range(2):
        pe[h, 0:D, :] = pg[h]
        pe[h, D:112, :] = ones
    give.wait()
    a, b = lp[core], rxa[...]
    top = jnp.maximum(a, b)
    cb[...] = top + jnp.log2(jnp.exp2(a - top) + jnp.exp2(b - top))
    sends = []
    for i in range(1, 16):
        cp = remote(cb, rxb.at[i], bs.at[i], br.at[i], at_plane(i))
        cp.start()
        sends.append(cp)
    rxb[0] = cb[...]
    for h in range(2):
        for k in range(0, HALF, 512):
            f = jnp.concatenate(
                [pg[h, :, k : k + 512].astype(F32), jnp.zeros((32, 512), F32)], axis=0
            )
            ptst[h * HALF + k : h * HALF + k + 512, :] = f.T.astype(BF)
    for cp in sends:
        cp.wait()
    top = rxb[0]
    for i in range(1, 16):
        top = jnp.maximum(top, rxb[i])
    total = jnp.exp2(rxb[0] - top)
    for i in range(1, 16):
        total = total + jnp.exp2(rxb[i] - top)
    lo[core] = top + jnp.log2(total)
    back = remote(lo.at[core], lo.at[core], ds.at[2], dr.at[2], other)
    back.start()
    own_log[...] = lo[core, :, mine] * LN2
    back.wait()

    row = lax.broadcasted_iota(jnp.int32, (32, 512), 0)
    for h in range(2):
        for k in range(0, HALF, 512):
            v = lo[h, :, k : k + 512] * (-1.0 / SCALE)
            hi = v.astype(BF).astype(F32)
            mid = (v - hi).astype(BF).astype(F32)
            low = v - hi - mid
            f = jnp.where(row == 0, hi, jnp.where(row == 1, mid, jnp.where(row == 2, low, 0.0)))
            ptst[h * HALF + k : h * HALF + k + 512, D:128] = f.T.astype(BF)

    first = lax.broadcasted_iota(jnp.int32, (16, 512), 0) == 0

    def owner(c, i):
        return pl.ds(pl.multiple_of(c * 1024 + lax.rem(z + i, 8) * 128, 128), 128)

    def sums(c):
        cps = []
        for near in ((4, 3, 5, 2), (6, 1, 7, 0)):
            uk = jnp.concatenate([ue[:, owner(c, i)] for i in near], axis=1)
            acc = jnp.zeros((112, 512), F32)
            for h in range(2):
                s = jnp.dot(ptst[h * HALF : h * HALF + HALF, :], uk, preferred_element_type=F32)
                e = jnp.exp2(s * SCALE).astype(BF)
                acc = acc + jnp.dot(pe[h], e, preferred_element_type=F32)
            tail = acc[D:112]
            hi = tail.astype(BF).astype(F32)
            parts = jnp.where(first, hi, tail - hi).astype(BF)
            for k, i in enumerate(near):
                at = slice(k * 128, k * 128 + 128)
                if i == 0:
                    w[c] = acc[0:104, at]
                    continue
                wb[c, i, 0:D] = acc[0:D, at].astype(BF)
                wb[c, i, D:112] = parts[:, at]
                cp = remote(wb.at[c, i], rxr.at[c, i], rs.at[c, i], rr.at[c, i], at_z(i))
                cp.start()
                cps.append(cp)
        return cps

    def finish(c):
        acc = w[c]
        for i in range(1, 8):
            acc = acc + rxr[c, i, 0:104].astype(F32)
        sums, mass = acc[0:D], acc[D : D + 1] + (acc[D + 1 : D + 2] - w[c, D + 1 : D + 2])
        u = ue[0:D, owner(c, 0)].astype(F32)
        fresh = ((sums + PRIOR_MASS * u) / (mass + PRIOR_MASS)).astype(BF)
        ga[c, 0, 0] = fresh[0:RA]
        g[c, 0, 0, 0] = fresh[RA:D]

    def along_z(c):
        cps = {}
        for j in range(1, 8):
            slot = g.at[c, 0, 0, j]
            cp = remote(g.at[c, 0, 0, 0], slot, zs.at[c, j], zr.at[c, j], at_z(ARRIVAL[j]))
            cp.start()
            cps[j] = cp
        return cps

    plane, ring = {}, {}

    def at_xy(dx, dh):
        return (yl, core, z, lax.rem(x + dx, 4), lax.rem(yh + dh, 2))

    def over_plane(c):
        plane[c] = []
        for n in (6, 2, 7, 5, 4, 3, 1):
            cp = remote(
                ga.at[c, 0, 0], ga.at[c, 0, n], as_.at[c, n], ar.at[c, n], at_xy(n % 4, n // 4)
            )
            cp.start()
            plane[c].append(cp)

    def hop(c, i, to):
        src, dst = i, (i + to) % 8
        j = ARRIVAL.index(dst)
        cp = remote(
            ga.at[c, ARRIVAL.index(src)], ga.at[c, j], rs_.at[c, j], rr_.at[c, j], at_z(to % 8)
        )
        cp.start()
        ring[c, dst] = cp

    def ring_step(c, n):
        if n == 0:
            for cp in plane[c]:
                cp.wait_recv()
            hop(c, 0, 1)
            hop(c, 0, -1)
        elif n < 4:
            up, down = n, 8 - n
            ring[c, up].wait_recv()
            if n < 3 or c == 0:
                hop(c, up, 1)
            ring[c, down].wait_recv()
            if n < 3 or c == 1:
                hop(c, down, -1)
        else:
            ring[c, 4].wait_recv()

    pushed = {}

    def push(c, n, dx, dh, to, rdx, rdh):
        js = pl.ds(n * GROUP, GROUP)
        cp = remote(
            g.at[c, dh, dx, js], g.at[c, rdh, rdx, js], gs.at[c, rdh, rdx, n], gr.at[c, rdh, rdx, n], to
        )
        cp.start()
        pushed[c, n, rdx, rdh] = cp

    def arrived(c, n, dx, dh):
        pushed[c, n, dx, dh].wait_recv()

    right, left = at_x(1), at_x(3)

    def y_last(c, n):
        return n % 2 == 0

    def relay(c, n, dh):
        if (c + n) % 2 == 0:
            arrived(c, n, 1, dh)
            push(c, n, 1, dh, right, 2, dh)
            arrived(c, n, 3, dh)
        else:
            arrived(c, n, 3, dh)
            push(c, n, 3, dh, left, 2, dh)
            arrived(c, n, 1, dh)

    def step1(c, n):
        for j in range(n * GROUP, n * GROUP + GROUP):
            if j:
                zc[c][j].wait_recv()
        push(c, n, 0, 0, across, 0, 1)
        push(c, n, 0, 0, right, 1, 0)
        push(c, n, 0, 0, left, 3, 0)

    def step2(c, n):
        relay(c, n, 0)
        if y_last(c, n):
            push(c, n, 1, 0, across, 1, 1)
            push(c, n, 3, 0, across, 3, 1)
        arrived(c, n, 0, 1)
        if not y_last(c, n):
            push(c, n, 0, 1, right, 1, 1)
            push(c, n, 0, 1, left, 3, 1)

    def step3(c, n):
        arrived(c, n, 2, 0)
        if y_last(c, n):
            push(c, n, 2, 0, across, 2, 1)
            arrived(c, n, 1, 1)
            arrived(c, n, 3, 1)
        else:
            relay(c, n, 1)

    def step4(c, n):
        arrived(c, n, 2, 1)

    zc = {}

    def begin(c):
        for cp in red[c]:
            cp.wait()
        finish(c)
        over_plane(c)
        zc[c] = along_z(c)

    events = [(4.9, 0, begin, (1,))]
    for c in range(2):
        for n in range(8 // GROUP):
            for k, step in enumerate((step1, step2, step3, step4)):
                events.append((5 * c + GROUP * n + 6 * k, k, step, (c, n)))
        for n in range(5):
            events.append((5 * c + 4.5 + 4 * n, 9, ring_step, (c, n)))
    events.sort(key=lambda e: (e[0], -e[1]))

    red = {}
    red[0] = sums(0)
    red[1] = sums(1)
    begin(0)
    for _, _, call, args in events:
        call(*args)
    for c in range(2):
        for cp in zc[c].values():
            cp.wait_send()
        for cp in plane[c]:
            cp.wait_send()
    for cp in list(pushed.values()) + list(ring.values()):
        cp.wait_send()


def widen_kernel(ga, g, log, out, log_out, buf, sem):
    mz, mx, mh = lax.axis_index("z"), lax.axis_index("x"), lax.axis_index("yh")
    cps = []
    for z in range(8):
        i = lax.rem(mz + 8 - z, 8)
        j = jnp.where(i == 0, 0, jnp.where(i <= 4, 2 * i - 1, 16 - 2 * i))
        for xx in range(4):
            dx = lax.rem(mx + 4 - xx, 4)
            for k in range(4):
                dh = lax.rem(mh + k // 2, 2)
                at = (z * 16 + xx * 4 + k) * 128
                buf[0:RA, at : at + 128] = ga[k % 2, j, dh * 4 + dx].astype(F32)
                buf[RA:D, at : at + 128] = g[k % 2, dh, dx, j].astype(F32)
        at = slice(z * 2048, z * 2048 + 2048)
        cp = pltpu.make_async_copy(buf.at[:, at], out.at[:, at], sem.at[z])
        cp.start()
        cps.append(cp)
    log_out[...] = log[0]
    for cp in cps:
        cp.wait()


def per_device(points, centroids):
    vmem = pl.BlockSpec(memory_space=pltpu.VMEM)
    dma = pltpu.SemaphoreType.DMA
    ga, g, own_log = pl.pallas_call(
        em_kernel,
        out_shape=[
            jax.ShapeDtypeStruct((2, 8, 8, RA, 128), BF),
            jax.ShapeDtypeStruct((2, 2, 4, 8, D - RA, 128), BF),
            jax.ShapeDtypeStruct((1, 128), F32),
        ],
        in_specs=[pl.BlockSpec(memory_space=pltpu.HBM)] * 2,
        out_specs=[vmem] * 3,
        scratch_shapes=[
            pltpu.VMEM((D, 128), BF),
            pltpu.VMEM((2, D, HALF), BF),
            pltpu.VMEM((D, 2048), BF),
            pltpu.VMEM((2048, 128), BF),
            pltpu.VMEM((128, 2048), BF),
            pltpu.VMEM((2 * HALF, 128), BF),
            pltpu.VMEM((2, 112, HALF), BF),
            pltpu.VMEM((2, 1, HALF), F32),
            pltpu.VMEM((1, HALF), F32),
            pltpu.VMEM((1, HALF), F32),
            pltpu.VMEM((16, 1, HALF), F32),
            pltpu.VMEM((2, 1, HALF), F32),
            pltpu.VMEM((2, 104, 128), F32),
            pltpu.VMEM((2, 8, 112, 128), BF),
            pltpu.VMEM((2, 8, 112, 128), BF),
            dma((17,)), dma((16,)), dma((16,)), dma((7,)), dma((7,)), dma((16,)), dma((16,)),
            dma((2, 8)), dma((2, 8)), dma((2, 8)), dma((2, 8)), dma((2, 2, 4, 8 // GROUP)), dma((2, 2, 4, 8 // GROUP)),
            dma((2, 8)), dma((2, 8)), dma((2, 8)), dma((2, 8)),
        ],
        compiler_params=pltpu.CompilerParams(
            collective_id=0, has_side_effects=True, vmem_limit_bytes=48 * 2**20
        ),
        name="em",
    )(points, centroids)
    return pl.pallas_call(
        widen_kernel,
        out_shape=[
            jax.ShapeDtypeStruct((D, 16384), F32),
            jax.ShapeDtypeStruct((128,), F32),
        ],
        in_specs=[vmem] * 3,
        out_specs=[pl.BlockSpec(memory_space=pltpu.HBM), vmem],
        scratch_shapes=[pltpu.VMEM((D, 16384), F32), dma((8,))],
        compiler_params=pltpu.CompilerParams(vmem_limit_bytes=12 * 2**20),
        name="widen",
    )(ga, g, own_log)


def solution(mesh):
    cube = Mesh(mesh.devices.reshape(2, 2, 8, 4, 2), AXES)
    return jax.shard_map(
        per_device,
        mesh=cube,
        in_specs=(P(None, AXES), P(None, ("yl", "core"))),
        out_specs=(P(None, ("yl", "core")), P(AXES)),
        check_vma=False,
    )
```

```python
import functools

import jax
import jax.numpy as jnp
from jax import lax
from jax.experimental import pallas as pl
from jax.experimental.pallas import tpu as pltpu
from jax.sharding import Mesh, PartitionSpec as P

TEMPER_SCALE = 10.0
PRIOR_MASS = 0.1
EPSILON = 1e-06
LOG2E = 1.4426950408889634
LN2 = 0.6931471805599453
SCALE = TEMPER_SCALE * LOG2E
AXES = ("yl", "core", "z", "x", "yh")
MESH = pl.DeviceIdType.MESH
D = 96
ARRIVAL = (0, 1, 7, 2, 6, 3, 5, 4)
GROUP = 2
RA = 32
HALF = 2048
BF = jnp.bfloat16
F32 = jnp.float32


def em_kernel(
    points, cents, ga, g, own_log,
    stage, pg, cu, ut, ue, ptst, pe, eb, lp, rxa, cb, rxb, lo, w, wb, rxr,
    cu_sem, ps, pr, ds, dr, bs, br, rs, rr, zs, zr, gs, gr, as_, ar, rs_, rr_,
):
    yl, core, z, x, yh = [lax.axis_index(a) for a in AXES]
    y = yh * 2 + yl
    chip = x * 4 + y

    def at_plane(i):
        tx, ty = lax.rem(x + i // 4, 4), lax.rem(y + i % 4, 4)
        return (lax.rem(ty, 2), core, z, tx, ty // 2)

    def at_z(i):
        return (yl, core, lax.rem(z + i, 8), x, yh)

    def at_x(i):
        return (yl, core, z, lax.rem(x + i, 4), yh)

    other = (yl, 1 - core, z, x, yh)
    across = (yl, core, z, x, 1 - yh)

    def remote(src, dst, s, r, to):
        return pltpu.make_async_remote_copy(
            src_ref=src, dst_ref=dst, send_sem=s, recv_sem=r, device_id=to, device_id_type=MESH
        )

    loads = []
    for c in range(2):
        for k in range(8):
            col = pl.multiple_of(k * 2048 + (x * 2 + yh) * 256 + c * 128, 128)
            n = c * 8 + k
            cp = pltpu.make_async_copy(
                cents.at[:, pl.ds(col, 128)], cu.at[:, n * 128 : n * 128 + 128], cu_sem.at[n]
            )
            cp.start()
            loads.append(cp)

    own = pltpu.make_async_copy(points, stage, cu_sem.at[16])
    own.start()
    barrier = pltpu.get_barrier_semaphore()
    peers = [at_plane(i) for i in range(1, 16)] + [other] + [at_z(i) for i in range(1, 8)]
    for to in peers:
        pl.semaphore_signal(barrier, inc=1, device_id=to, device_id_type=MESH)
    for cp in loads:
        cp.wait()
    ue[D:128, :] = jnp.where(
        lax.broadcasted_iota(jnp.int32, (32, 2048), 0) < 3, 1.0, 0.0
    ).astype(BF)
    for k in range(0, 2048, 512):
        f = cu[:, k : k + 512].astype(F32)
        u = (f * lax.rsqrt(jnp.sum(f * f, axis=0, keepdims=True) + EPSILON)).astype(BF)
        ue[0:D, k : k + 512] = u
        full = jnp.concatenate([u.astype(F32), jnp.zeros((32, 512), F32)], axis=0)
        ut[k : k + 512, :] = full.T.astype(BF)
    pl.semaphore_wait(barrier, len(peers))

    mine = pl.ds(pl.multiple_of(chip * 128, 128), 128)
    order = (1, 2, 3, 4, 5, 6, 7, 12, 13, 14, 15, 8, 9, 10, 11)
    own.wait()
    sends = {}
    for i in order:
        cp = remote(stage, pg.at[core, :, mine], ps.at[i], pr.at[i], at_plane(i))
        cp.start()
        sends[i] = cp
    pg[core, :, mine] = stage[...]

    def column(k):
        return pl.ds(pl.multiple_of(lax.rem(x + 4 - k, 4) * 512, 512), 512)

    def stats(h, k):
        pts = pg[h, :, column(k)]
        top = jnp.full((8, 512), -1e30, F32)
        total = jnp.zeros((8, 512), F32)
        for r in range(0, 2048, 128):
            s = jnp.dot(ut[r : r + 128, 0:D], pts, preferred_element_type=F32)
            s = s.reshape(16, 8, 512)
            new = jnp.maximum(top, jnp.max(s, axis=0))
            e = jnp.exp2((s - new[None]) * SCALE)
            total = total * jnp.exp2((top - new) * SCALE) + jnp.sum(e, axis=0)
            top = new
        best = jnp.max(top, axis=0, keepdims=True)
        sums = jnp.sum(total * jnp.exp2((top - best) * SCALE), axis=0, keepdims=True)
        lp[h, :, column(k)] = best * SCALE + jnp.log2(sums)

    swaps, before = [], None
    for n, k in enumerate((0, 1, 3, 2)):
        for i in range(4 * k, 4 * k + 4):
            if i:
                sends[i].wait_recv()
        part = pg.at[core, :, column(k)]
        swap = remote(part, part, ds.at[3 + n], dr.at[3 + n], other)
        swap.start()
        if before is not None:
            swaps[-1].wait_recv()
            stats(1 - core, before)
        swaps.append(swap)
        stats(core, k)
        before = k
    swaps[-1].wait_recv()
    stats(1 - core, before)
    for cp in list(sends.values()) + swaps:
        cp.wait_send()

    give = remote(lp.at[1 - core], rxa, ds.at[1], dr.at[1], other)
    give.start()
    give.wait()
    a, b = lp[core], rxa[...]
    top = jnp.maximum(a, b)
    cb[...] = top + jnp.log2(jnp.exp2(a - top) + jnp.exp2(b - top))
    sends = []
    for i in range(1, 16):
        cp = remote(cb, rxb.at[i], bs.at[i], br.at[i], at_plane(i))
        cp.start()
        sends.append(cp)
    rxb[0] = cb[...]
    for h in range(2):
        for k in range(0, HALF, 512):
            f = jnp.concatenate(
                [pg[h, :, k : k + 512].astype(F32), jnp.zeros((32, 512), F32)], axis=0
            )
            ptst[h * HALF + k : h * HALF + k + 512, :] = f.T.astype(BF)
    row = lax.broadcasted_iota(jnp.int32, (32, 512), 0)
    for h in range(2):
        for k in range(0, HALF, 512):
            v = lp[h, :, k : k + 512] * (-1.0 / SCALE)
            hi = v.astype(BF).astype(F32)
            mid = (v - hi).astype(BF).astype(F32)
            low = v - hi - mid
            f = jnp.where(row == 0, hi, jnp.where(row == 1, mid, jnp.where(row == 2, low, 0.0)))
            ptst[h * HALF + k : h * HALF + k + 512, D:128] = f.T.astype(BF)

    def owner(c, i):
        return pl.ds(pl.multiple_of(c * 1024 + lax.rem(z + i, 8) * 128, 128), 128)

    near = ((4, 3, 5, 2), (6, 1, 7, 0))
    for c in range(2):
        for q in range(2):
            uk = jnp.concatenate([ue[:, owner(c, i)] for i in near[q]], axis=1)
            for h in range(2):
                at = slice(h * HALF, h * HALF + HALF)
                s = jnp.dot(ptst[at, :], uk, preferred_element_type=F32)
                eb[c, q, at, :] = jnp.exp2(s * SCALE).astype(BF)
    for cp in sends:
        cp.wait()
    top = rxb[0]
    for i in range(1, 16):
        top = jnp.maximum(top, rxb[i])
    total = jnp.exp2(rxb[0] - top)
    for i in range(1, 16):
        total = total + jnp.exp2(rxb[i] - top)
    lo[core] = top + jnp.log2(total)
    back = remote(lo.at[core], lo.at[core], ds.at[2], dr.at[2], other)
    back.start()
    own_log[...] = lo[core, :, mine] * LN2
    back.wait()

    mrow = lax.broadcasted_iota(jnp.int32, (16, 512), 0)
    for h in range(2):
        for k in range(0, HALF, 512):
            at = slice(k, k + 512)
            f = jnp.exp2(lp[h, :, at] - lo[h, :, at])
            v = pg[h, :, at].astype(F32) * f
            hi = v.astype(BF)
            pe[h, 0:D, at] = hi
            pe[h, D : 2 * D, at] = (v - hi.astype(F32)).astype(BF)
            fh = f.astype(BF).astype(F32)
            pe[h, 2 * D : 208, at] = jnp.where(
                mrow == 0, fh, jnp.where(mrow == 1, f - fh, 0.0)
            ).astype(BF)

    def sums(c):
        cps = []
        for q in range(2):
            acc = jnp.dot(pe[0], eb[c, q, 0:HALF, :], preferred_element_type=F32)
            acc = acc + jnp.dot(pe[1], eb[c, q, HALF : 2 * HALF, :], preferred_element_type=F32)
            total = acc[0:D] + acc[D : 2 * D]
            mass = acc[2 * D : 2 * D + 1] + acc[2 * D + 1 : 2 * D + 2]
            hi = mass.astype(BF).astype(F32)
            parts = jnp.where(mrow == 0, hi, jnp.where(mrow == 1, mass - hi, 0.0)).astype(BF)
            for k, i in enumerate(near[q]):
                at = slice(k * 128, k * 128 + 128)
                if i == 0:
                    w[c, 0:D] = total[:, at]
                    w[c, D:104] = jnp.broadcast_to(mass[:, at], (8, 128))
                    continue
                wb[c, i, 0:D] = total[:, at].astype(BF)
                wb[c, i, D:112] = parts[:, at]
                cp = remote(wb.at[c, i], rxr.at[c, i], rs.at[c, i], rr.at[c, i], at_z(i))
                cp.start()
                cps.append(cp)
        return cps

    def finish(c):
        acc = w[c]
        for i in range(1, 8):
            acc = acc + rxr[c, i, 0:104].astype(F32)
        sums, mass = acc[0:D], acc[D : D + 1] + (acc[D + 1 : D + 2] - w[c, D + 1 : D + 2])
        u = ue[0:D, owner(c, 0)].astype(F32)
        fresh = ((sums + PRIOR_MASS * u) / (mass + PRIOR_MASS)).astype(BF)
        ga[c, 0, 0] = fresh[0:RA]
        g[c, 0, 0, 0] = fresh[RA:D]

    def along_z(c):
        cps = {}
        for j in range(1, 8):
            slot = g.at[c, 0, 0, j]
            cp = remote(g.at[c, 0, 0, 0], slot, zs.at[c, j], zr.at[c, j], at_z(ARRIVAL[j]))
            cp.start()
            cps[j] = cp
        return cps

    plane, ring = {}, {}

    def at_xy(dx, dh):
        return (yl, core, z, lax.rem(x + dx, 4), lax.rem(yh + dh, 2))

    def over_plane(c):
        plane[c] = []
        for n in (6, 2, 7, 5, 4, 3, 1):
            cp = remote(
                ga.at[c, 0, 0], ga.at[c, 0, n], as_.at[c, n], ar.at[c, n], at_xy(n % 4, n // 4)
            )
            cp.start()
            plane[c].append(cp)

    def hop(c, i, to):
        src, dst = i, (i + to) % 8
        j = ARRIVAL.index(dst)
        cp = remote(
            ga.at[c, ARRIVAL.index(src)], ga.at[c, j], rs_.at[c, j], rr_.at[c, j], at_z(to % 8)
        )
        cp.start()
        ring[c, dst] = cp

    def ring_step(c, n):
        if n == 0:
            for cp in plane[c]:
                cp.wait_recv()
            hop(c, 0, 1)
            hop(c, 0, -1)
        elif n < 4:
            up, down = n, 8 - n
            ring[c, up].wait_recv()
            if n < 3 or c == 0:
                hop(c, up, 1)
            ring[c, down].wait_recv()
            if n < 3 or c == 1:
                hop(c, down, -1)
        else:
            ring[c, 4].wait_recv()

    pushed = {}

    def push(c, n, dx, dh, to, rdx, rdh):
        js = pl.ds(n * GROUP, GROUP)
        cp = remote(
            g.at[c, dh, dx, js], g.at[c, rdh, rdx, js], gs.at[c, rdh, rdx, n], gr.at[c, rdh, rdx, n], to
        )
        cp.start()
        pushed[c, n, rdx, rdh] = cp

    def arrived(c, n, dx, dh):
        pushed[c, n, dx, dh].wait_recv()

    right, left = at_x(1), at_x(3)

    def y_last(c, n):
        return n % 2 == 0

    def relay(c, n, dh):
        if (c + n) % 2 == 0:
            arrived(c, n, 1, dh)
            push(c, n, 1, dh, right, 2, dh)
            arrived(c, n, 3, dh)
        else:
            arrived(c, n, 3, dh)
            push(c, n, 3, dh, left, 2, dh)
            arrived(c, n, 1, dh)

    def step1(c, n):
        for j in range(n * GROUP, n * GROUP + GROUP):
            if j:
                zc[c][j].wait_recv()
        push(c, n, 0, 0, across, 0, 1)
        push(c, n, 0, 0, right, 1, 0)
        push(c, n, 0, 0, left, 3, 0)

    def step2(c, n):
        relay(c, n, 0)
        if y_last(c, n):
            push(c, n, 1, 0, across, 1, 1)
            push(c, n, 3, 0, across, 3, 1)
        arrived(c, n, 0, 1)
        if not y_last(c, n):
            push(c, n, 0, 1, right, 1, 1)
            push(c, n, 0, 1, left, 3, 1)

    def step3(c, n):
        arrived(c, n, 2, 0)
        if y_last(c, n):
            push(c, n, 2, 0, across, 2, 1)
            arrived(c, n, 1, 1)
            arrived(c, n, 3, 1)
        else:
            relay(c, n, 1)

    def step4(c, n):
        arrived(c, n, 2, 1)

    zc = {}

    def begin(c):
        for cp in red[c]:
            cp.wait()
        finish(c)
        over_plane(c)
        zc[c] = along_z(c)

    events = [(4.9, 0, begin, (1,))]
    for c in range(2):
        for n in range(8 // GROUP):
            for k, step in enumerate((step1, step2, step3, step4)):
                events.append((5 * c + GROUP * n + 6 * k, k, step, (c, n)))
        for n in range(5):
            events.append((5 * c + 4.5 + 4 * n, 9, ring_step, (c, n)))
    events.sort(key=lambda e: (e[0], -e[1]))

    red = {}
    red[0] = sums(0)
    red[1] = sums(1)
    begin(0)
    for _, _, call, args in events:
        call(*args)
    for c in range(2):
        for cp in zc[c].values():
            cp.wait_send()
        for cp in plane[c]:
            cp.wait_send()
    for cp in list(pushed.values()) + list(ring.values()):
        cp.wait_send()


def widen_kernel(ga, g, log, out, log_out, buf, sem):
    mz, mx, mh = lax.axis_index("z"), lax.axis_index("x"), lax.axis_index("yh")
    cps = []
    for z in range(8):
        i = lax.rem(mz + 8 - z, 8)
        j = jnp.where(i == 0, 0, jnp.where(i <= 4, 2 * i - 1, 16 - 2 * i))
        for xx in range(4):
            dx = lax.rem(mx + 4 - xx, 4)
            for k in range(4):
                dh = lax.rem(mh + k // 2, 2)
                at = (z * 16 + xx * 4 + k) * 128
                buf[0:RA, at : at + 128] = ga[k % 2, j, dh * 4 + dx].astype(F32)
                buf[RA:D, at : at + 128] = g[k % 2, dh, dx, j].astype(F32)
        at = slice(z * 2048, z * 2048 + 2048)
        cp = pltpu.make_async_copy(buf.at[:, at], out.at[:, at], sem.at[z])
        cp.start()
        cps.append(cp)
    log_out[...] = log[0]
    for cp in cps:
        cp.wait()


def per_device(points, centroids):
    vmem = pl.BlockSpec(memory_space=pltpu.VMEM)
    dma = pltpu.SemaphoreType.DMA
    ga, g, own_log = pl.pallas_call(
        em_kernel,
        out_shape=[
            jax.ShapeDtypeStruct((2, 8, 8, RA, 128), BF),
            jax.ShapeDtypeStruct((2, 2, 4, 8, D - RA, 128), BF),
            jax.ShapeDtypeStruct((1, 128), F32),
        ],
        in_specs=[pl.BlockSpec(memory_space=pltpu.HBM)] * 2,
        out_specs=[vmem] * 3,
        scratch_shapes=[
            pltpu.VMEM((D, 128), BF),
            pltpu.VMEM((2, D, HALF), BF),
            pltpu.VMEM((D, 2048), BF),
            pltpu.VMEM((2048, 128), BF),
            pltpu.VMEM((128, 2048), BF),
            pltpu.VMEM((2 * HALF, 128), BF),
            pltpu.VMEM((2, 208, HALF), BF),
            pltpu.VMEM((2, 2, 2 * HALF, 512), BF),
            pltpu.VMEM((2, 1, HALF), F32),
            pltpu.VMEM((1, HALF), F32),
            pltpu.VMEM((1, HALF), F32),
            pltpu.VMEM((16, 1, HALF), F32),
            pltpu.VMEM((2, 1, HALF), F32),
            pltpu.VMEM((2, 104, 128), F32),
            pltpu.VMEM((2, 8, 112, 128), BF),
            pltpu.VMEM((2, 8, 112, 128), BF),
            dma((17,)), dma((16,)), dma((16,)), dma((7,)), dma((7,)), dma((16,)), dma((16,)),
            dma((2, 8)), dma((2, 8)), dma((2, 8)), dma((2, 8)), dma((2, 2, 4, 8 // GROUP)), dma((2, 2, 4, 8 // GROUP)),
            dma((2, 8)), dma((2, 8)), dma((2, 8)), dma((2, 8)),
        ],
        compiler_params=pltpu.CompilerParams(
            collective_id=0, has_side_effects=True, vmem_limit_bytes=48 * 2**20
        ),
        name="em",
    )(points, centroids)
    return pl.pallas_call(
        widen_kernel,
        out_shape=[
            jax.ShapeDtypeStruct((D, 16384), F32),
            jax.ShapeDtypeStruct((128,), F32),
        ],
        in_specs=[vmem] * 3,
        out_specs=[pl.BlockSpec(memory_space=pltpu.HBM), vmem],
        scratch_shapes=[pltpu.VMEM((D, 16384), F32), dma((8,))],
        compiler_params=pltpu.CompilerParams(vmem_limit_bytes=12 * 2**20),
        name="widen",
    )(ga, g, own_log)


def solution(mesh):
    cube = Mesh(mesh.devices.reshape(2, 2, 8, 4, 2), AXES)
    return jax.shard_map(
        per_device,
        mesh=cube,
        in_specs=(P(None, AXES), P(None, ("yl", "core"))),
        out_specs=(P(None, ("yl", "core")), P(AXES)),
        check_vma=False,
    )
```

```python
import functools

import jax
import jax.numpy as jnp
from jax import lax
from jax.experimental import pallas as pl
from jax.experimental.pallas import tpu as pltpu
from jax.sharding import Mesh, PartitionSpec as P

TEMPER_SCALE = 10.0
PRIOR_MASS = 0.1
EPSILON = 1e-06
LOG2E = 1.4426950408889634
LN2 = 0.6931471805599453
SCALE = TEMPER_SCALE * LOG2E
AXES = ("yl", "core", "z", "x", "yh")
MESH = pl.DeviceIdType.MESH
D = 96
ARRIVAL = (0, 1, 7, 2, 6, 3, 5, 4)
GROUP = 2
RA = 32
HALF = 2048
BF = jnp.bfloat16
F32 = jnp.float32


def em_kernel(
    points, cents, ga, g, own_log,
    stage, pg, cu, ut, ue, ptst, pe, eb, lp, rxa, cb, rxb, lo, w, wb, rxr,
    cu_sem, ps, pr, ds, dr, bs, br, rs, rr, zs, zr, gs, gr, as_, ar, rs_, rr_,
):
    yl, core, z, x, yh = [lax.axis_index(a) for a in AXES]
    y = yh * 2 + yl
    chip = x * 4 + y

    def at_plane(i):
        tx, ty = lax.rem(x + i // 4, 4), lax.rem(y + i % 4, 4)
        return (lax.rem(ty, 2), core, z, tx, ty // 2)

    def at_z(i):
        return (yl, core, lax.rem(z + i, 8), x, yh)

    def at_x(i):
        return (yl, core, z, lax.rem(x + i, 4), yh)

    other = (yl, 1 - core, z, x, yh)
    across = (yl, core, z, x, 1 - yh)

    def remote(src, dst, s, r, to):
        return pltpu.make_async_remote_copy(
            src_ref=src, dst_ref=dst, send_sem=s, recv_sem=r, device_id=to, device_id_type=MESH
        )

    loads = []
    for c in range(2):
        for k in range(8):
            col = pl.multiple_of(k * 2048 + (x * 2 + yh) * 256 + c * 128, 128)
            n = c * 8 + k
            cp = pltpu.make_async_copy(
                cents.at[:, pl.ds(col, 128)], cu.at[:, n * 128 : n * 128 + 128], cu_sem.at[n]
            )
            cp.start()
            loads.append(cp)

    own = pltpu.make_async_copy(points, stage, cu_sem.at[16])
    own.start()
    barrier = pltpu.get_barrier_semaphore()
    peers = [at_plane(i) for i in range(1, 16)] + [other] + [at_z(i) for i in range(1, 8)]
    for to in peers:
        pl.semaphore_signal(barrier, inc=1, device_id=to, device_id_type=MESH)
    for cp in loads:
        cp.wait()
    ue[D:128, :] = jnp.where(
        lax.broadcasted_iota(jnp.int32, (32, 2048), 0) < 3, 1.0, 0.0
    ).astype(BF)
    for k in range(0, 2048, 512):
        f = cu[:, k : k + 512].astype(F32)
        u = (f * lax.rsqrt(jnp.sum(f * f, axis=0, keepdims=True) + EPSILON)).astype(BF)
        ue[0:D, k : k + 512] = u
        full = jnp.concatenate([u.astype(F32), jnp.zeros((32, 512), F32)], axis=0)
        ut[k : k + 512, :] = full.T.astype(BF)
    pl.semaphore_wait(barrier, len(peers))

    mine = pl.ds(pl.multiple_of(chip * 128, 128), 128)
    order = (1, 2, 3, 4, 5, 6, 7, 12, 13, 14, 15, 8, 9, 10, 11)
    own.wait()
    sends = {}
    for i in order:
        cp = remote(stage, pg.at[core, :, mine], ps.at[i], pr.at[i], at_plane(i))
        cp.start()
        sends[i] = cp
    pg[core, :, mine] = stage[...]

    def column(k):
        return pl.ds(pl.multiple_of(lax.rem(x + 4 - k, 4) * 512, 512), 512)

    def stats(h, k):
        pts = pg[h, :, column(k)]
        top = jnp.full((8, 512), -1e30, F32)
        total = jnp.zeros((8, 512), F32)
        for r in range(0, 2048, 128):
            s = jnp.dot(ut[r : r + 128, 0:D], pts, preferred_element_type=F32)
            s = s.reshape(16, 8, 512)
            new = jnp.maximum(top, jnp.max(s, axis=0))
            e = jnp.exp2((s - new[None]) * SCALE)
            total = total * jnp.exp2((top - new) * SCALE) + jnp.sum(e, axis=0)
            top = new
        best = jnp.max(top, axis=0, keepdims=True)
        sums = jnp.sum(total * jnp.exp2((top - best) * SCALE), axis=0, keepdims=True)
        lp[h, :, column(k)] = best * SCALE + jnp.log2(sums)

    swaps, before = [], None
    for n, k in enumerate((0, 1, 3, 2)):
        for i in range(4 * k, 4 * k + 4):
            if i:
                sends[i].wait_recv()
        part = pg.at[core, :, column(k)]
        swap = remote(part, part, ds.at[3 + n], dr.at[3 + n], other)
        swap.start()
        if before is not None:
            swaps[-1].wait_recv()
            stats(1 - core, before)
        swaps.append(swap)
        stats(core, k)
        before = k
    swaps[-1].wait_recv()
    stats(1 - core, before)
    for cp in list(sends.values()) + swaps:
        cp.wait_send()

    give = remote(lp.at[1 - core], rxa, ds.at[1], dr.at[1], other)
    give.start()
    give.wait()
    a, b = lp[core], rxa[...]
    top = jnp.maximum(a, b)
    cb[...] = top + jnp.log2(jnp.exp2(a - top) + jnp.exp2(b - top))
    sends = []
    for i in range(1, 16):
        cp = remote(cb, rxb.at[i], bs.at[i], br.at[i], at_plane(i))
        cp.start()
        sends.append(cp)
    rxb[0] = cb[...]
    for h in range(2):
        for k in range(0, HALF, 512):
            f = jnp.concatenate(
                [pg[h, :, k : k + 512].astype(F32), jnp.zeros((32, 512), F32)], axis=0
            )
            ptst[h * HALF + k : h * HALF + k + 512, :] = f.T.astype(BF)
    row = lax.broadcasted_iota(jnp.int32, (32, 512), 0)
    for h in range(2):
        for k in range(0, HALF, 512):
            v = lp[h, :, k : k + 512] * (-1.0 / SCALE)
            hi = v.astype(BF).astype(F32)
            mid = (v - hi).astype(BF).astype(F32)
            low = v - hi - mid
            f = jnp.where(row == 0, hi, jnp.where(row == 1, mid, jnp.where(row == 2, low, 0.0)))
            ptst[h * HALF + k : h * HALF + k + 512, D:128] = f.T.astype(BF)

    def owner(c, i):
        return pl.ds(pl.multiple_of(c * 1024 + lax.rem(z + i, 8) * 128, 128), 128)

    near = ((4, 3, 5, 2), (6, 1, 7, 0))

    def weigh(c, q):
        uk = jnp.concatenate([ue[:, owner(c, i)] for i in near[q]], axis=1)
        for h in range(2):
            at = slice(h * HALF, h * HALF + HALF)
            s = jnp.dot(ptst[at, :], uk, preferred_element_type=F32)
            eb[c, q, at, :] = jnp.exp2(s * SCALE).astype(BF)

    for c, q in ((0, 0), (0, 1), (1, 0)):
        weigh(c, q)
    for cp in sends:
        cp.wait()
    top = rxb[0]
    for i in range(1, 16):
        top = jnp.maximum(top, rxb[i])
    total = jnp.exp2(rxb[0] - top)
    for i in range(1, 16):
        total = total + jnp.exp2(rxb[i] - top)
    lo[core] = top + jnp.log2(total)
    back = remote(lo.at[core], lo.at[core], ds.at[2], dr.at[2], other)
    back.start()
    own_log[...] = lo[core, :, mine] * LN2
    back.wait()

    mrow = lax.broadcasted_iota(jnp.int32, (16, 512), 0)
    for h in range(2):
        for k in range(0, HALF, 512):
            at = slice(k, k + 512)
            f = jnp.exp2(lp[h, :, at] - lo[h, :, at])
            v = pg[h, :, at].astype(F32) * f
            hi = v.astype(BF)
            pe[h, 0:D, at] = hi
            pe[h, D : 2 * D, at] = (v - hi.astype(F32)).astype(BF)
            fh = f.astype(BF).astype(F32)
            pe[h, 2 * D : 208, at] = jnp.where(
                mrow == 0, fh, jnp.where(mrow == 1, f - fh, 0.0)
            ).astype(BF)

    def sums(c):
        cps = []
        for q in range(2):
            if c == 1 and q == 1:
                weigh(c, q)
            acc = jnp.dot(pe[0], eb[c, q, 0:HALF, :], preferred_element_type=F32)
            acc = acc + jnp.dot(pe[1], eb[c, q, HALF : 2 * HALF, :], preferred_element_type=F32)
            total = acc[0:D] + acc[D : 2 * D]
            mass = acc[2 * D : 2 * D + 1] + acc[2 * D + 1 : 2 * D + 2]
            hi = mass.astype(BF).astype(F32)
            parts = jnp.where(mrow == 0, hi, jnp.where(mrow == 1, mass - hi, 0.0)).astype(BF)
            for k, i in enumerate(near[q]):
                at = slice(k * 128, k * 128 + 128)
                if i == 0:
                    w[c, 0:D] = total[:, at]
                    w[c, D:104] = jnp.broadcast_to(mass[:, at], (8, 128))
                    continue
                wb[c, i, 0:D] = total[:, at].astype(BF)
                wb[c, i, D:112] = parts[:, at]
                cp = remote(wb.at[c, i], rxr.at[c, i], rs.at[c, i], rr.at[c, i], at_z(i))
                cp.start()
                cps.append(cp)
        return cps

    def finish(c):
        acc = w[c]
        for i in range(1, 8):
            acc = acc + rxr[c, i, 0:104].astype(F32)
        sums, mass = acc[0:D], acc[D : D + 1] + (acc[D + 1 : D + 2] - w[c, D + 1 : D + 2])
        u = ue[0:D, owner(c, 0)].astype(F32)
        fresh = ((sums + PRIOR_MASS * u) / (mass + PRIOR_MASS)).astype(BF)
        ga[c, 0, 0] = fresh[0:RA]
        g[c, 0, 0, 0] = fresh[RA:D]

    def along_z(c):
        cps = {}
        for j in range(1, 8):
            slot = g.at[c, 0, 0, j]
            cp = remote(g.at[c, 0, 0, 0], slot, zs.at[c, j], zr.at[c, j], at_z(ARRIVAL[j]))
            cp.start()
            cps[j] = cp
        return cps

    plane, ring = {}, {}

    def at_xy(dx, dh):
        return (yl, core, z, lax.rem(x + dx, 4), lax.rem(yh + dh, 2))

    def over_plane(c):
        plane[c] = []
        for n in (6, 2, 7, 5, 4, 3, 1):
            cp = remote(
                ga.at[c, 0, 0], ga.at[c, 0, n], as_.at[c, n], ar.at[c, n], at_xy(n % 4, n // 4)
            )
            cp.start()
            plane[c].append(cp)

    def hop(c, i, to):
        src, dst = i, (i + to) % 8
        j = ARRIVAL.index(dst)
        cp = remote(
            ga.at[c, ARRIVAL.index(src)], ga.at[c, j], rs_.at[c, j], rr_.at[c, j], at_z(to % 8)
        )
        cp.start()
        ring[c, dst] = cp

    def ring_step(c, n):
        if n == 0:
            for cp in plane[c]:
                cp.wait_recv()
            hop(c, 0, 1)
            hop(c, 0, -1)
        elif n < 4:
            up, down = n, 8 - n
            ring[c, up].wait_recv()
            if n < 3 or c == 0:
                hop(c, up, 1)
            ring[c, down].wait_recv()
            if n < 3 or c == 1:
                hop(c, down, -1)
        else:
            ring[c, 4].wait_recv()

    pushed = {}

    def push(c, n, dx, dh, to, rdx, rdh):
        js = pl.ds(n * GROUP, GROUP)
        cp = remote(
            g.at[c, dh, dx, js], g.at[c, rdh, rdx, js], gs.at[c, rdh, rdx, n], gr.at[c, rdh, rdx, n], to
        )
        cp.start()
        pushed[c, n, rdx, rdh] = cp

    def arrived(c, n, dx, dh):
        pushed[c, n, dx, dh].wait_recv()

    right, left = at_x(1), at_x(3)

    def y_last(c, n):
        return n % 2 == 0

    def relay(c, n, dh):
        if (c + n) % 2 == 0:
            arrived(c, n, 1, dh)
            push(c, n, 1, dh, right, 2, dh)
            arrived(c, n, 3, dh)
        else:
            arrived(c, n, 3, dh)
            push(c, n, 3, dh, left, 2, dh)
            arrived(c, n, 1, dh)

    def step1(c, n):
        for j in range(n * GROUP, n * GROUP + GROUP):
            if j:
                zc[c][j].wait_recv()
        push(c, n, 0, 0, across, 0, 1)
        push(c, n, 0, 0, right, 1, 0)
        push(c, n, 0, 0, left, 3, 0)

    def step2(c, n):
        relay(c, n, 0)
        if y_last(c, n):
            push(c, n, 1, 0, across, 1, 1)
            push(c, n, 3, 0, across, 3, 1)
        arrived(c, n, 0, 1)
        if not y_last(c, n):
            push(c, n, 0, 1, right, 1, 1)
            push(c, n, 0, 1, left, 3, 1)

    def step3(c, n):
        arrived(c, n, 2, 0)
        if y_last(c, n):
            push(c, n, 2, 0, across, 2, 1)
            arrived(c, n, 1, 1)
            arrived(c, n, 3, 1)
        else:
            relay(c, n, 1)

    def step4(c, n):
        arrived(c, n, 2, 1)

    zc = {}

    def begin(c):
        for cp in red[c]:
            cp.wait()
        finish(c)
        over_plane(c)
        zc[c] = along_z(c)

    events = [(4.9, 0, begin, (1,))]
    for c in range(2):
        for n in range(8 // GROUP):
            for k, step in enumerate((step1, step2, step3, step4)):
                events.append((5 * c + GROUP * n + 6 * k, k, step, (c, n)))
        for n in range(5):
            events.append((5 * c + 4.5 + 4 * n, 9, ring_step, (c, n)))
    events.sort(key=lambda e: (e[0], -e[1]))

    red = {}
    red[0] = sums(0)
    red[1] = sums(1)
    begin(0)
    for _, _, call, args in events:
        call(*args)
    for c in range(2):
        for cp in zc[c].values():
            cp.wait_send()
        for cp in plane[c]:
            cp.wait_send()
    for cp in list(pushed.values()) + list(ring.values()):
        cp.wait_send()


def widen_kernel(ga, g, log, out, log_out, buf, sem):
    mz, mx, mh = lax.axis_index("z"), lax.axis_index("x"), lax.axis_index("yh")
    cps = []
    for z in range(8):
        i = lax.rem(mz + 8 - z, 8)
        j = jnp.where(i == 0, 0, jnp.where(i <= 4, 2 * i - 1, 16 - 2 * i))
        for xx in range(4):
            dx = lax.rem(mx + 4 - xx, 4)
            for k in range(4):
                dh = lax.rem(mh + k // 2, 2)
                at = (z * 16 + xx * 4 + k) * 128
                buf[0:RA, at : at + 128] = ga[k % 2, j, dh * 4 + dx].astype(F32)
                buf[RA:D, at : at + 128] = g[k % 2, dh, dx, j].astype(F32)
        at = slice(z * 2048, z * 2048 + 2048)
        cp = pltpu.make_async_copy(buf.at[:, at], out.at[:, at], sem.at[z])
        cp.start()
        cps.append(cp)
    log_out[...] = log[0]
    for cp in cps:
        cp.wait()


def per_device(points, centroids):
    vmem = pl.BlockSpec(memory_space=pltpu.VMEM)
    dma = pltpu.SemaphoreType.DMA
    ga, g, own_log = pl.pallas_call(
        em_kernel,
        out_shape=[
            jax.ShapeDtypeStruct((2, 8, 8, RA, 128), BF),
            jax.ShapeDtypeStruct((2, 2, 4, 8, D - RA, 128), BF),
            jax.ShapeDtypeStruct((1, 128), F32),
        ],
        in_specs=[pl.BlockSpec(memory_space=pltpu.HBM)] * 2,
        out_specs=[vmem] * 3,
        scratch_shapes=[
            pltpu.VMEM((D, 128), BF),
            pltpu.VMEM((2, D, HALF), BF),
            pltpu.VMEM((D, 2048), BF),
            pltpu.VMEM((2048, 128), BF),
            pltpu.VMEM((128, 2048), BF),
            pltpu.VMEM((2 * HALF, 128), BF),
            pltpu.VMEM((2, 208, HALF), BF),
            pltpu.VMEM((2, 2, 2 * HALF, 512), BF),
            pltpu.VMEM((2, 1, HALF), F32),
            pltpu.VMEM((1, HALF), F32),
            pltpu.VMEM((1, HALF), F32),
            pltpu.VMEM((16, 1, HALF), F32),
            pltpu.VMEM((2, 1, HALF), F32),
            pltpu.VMEM((2, 104, 128), F32),
            pltpu.VMEM((2, 8, 112, 128), BF),
            pltpu.VMEM((2, 8, 112, 128), BF),
            dma((17,)), dma((16,)), dma((16,)), dma((7,)), dma((7,)), dma((16,)), dma((16,)),
            dma((2, 8)), dma((2, 8)), dma((2, 8)), dma((2, 8)), dma((2, 2, 4, 8 // GROUP)), dma((2, 2, 4, 8 // GROUP)),
            dma((2, 8)), dma((2, 8)), dma((2, 8)), dma((2, 8)),
        ],
        compiler_params=pltpu.CompilerParams(
            collective_id=0, has_side_effects=True, vmem_limit_bytes=48 * 2**20
        ),
        name="em",
    )(points, centroids)
    return pl.pallas_call(
        widen_kernel,
        out_shape=[
            jax.ShapeDtypeStruct((D, 16384), F32),
            jax.ShapeDtypeStruct((128,), F32),
        ],
        in_specs=[vmem] * 3,
        out_specs=[pl.BlockSpec(memory_space=pltpu.HBM), vmem],
        scratch_shapes=[pltpu.VMEM((D, 16384), F32), dma((8,))],
        compiler_params=pltpu.CompilerParams(vmem_limit_bytes=12 * 2**20),
        name="widen",
    )(ga, g, own_log)


def solution(mesh):
    cube = Mesh(mesh.devices.reshape(2, 2, 8, 4, 2), AXES)
    return jax.shard_map(
        per_device,
        mesh=cube,
        in_specs=(P(None, AXES), P(None, ("yl", "core"))),
        out_specs=(P(None, ("yl", "core")), P(AXES)),
        check_vma=False,
    )
```
